128 devices in a mesh: rep: 64 (over z, y, x), fsdp: 2 (over core).
Axes of the slice: x: 4, y: 4, z: 4, core: 2. Of those that a mesh axis runs over, the one named last changes fastest.
Arguments:
- acts: bfloat16 [131072, 5120], P(('rep', 'fsdp')), may hold values from -24 to 24
- cotangent: bfloat16 [131072, 512], P(('rep', 'fsdp')), may hold values from -0.125 to 0.125
- weight: bfloat16 [5120, 512], P('fsdp'), may hold values from -0.078125 to 0.078125
- momentum: float32 [64, 5120, 512], P('rep', 'fsdp'), may hold values from -6 to 6
Outputs:
- new_momentum: float32 [64, 5120, 512], P('rep', 'fsdp')
- update: float32 [5120, 512], P('fsdp')
- new_weight: bfloat16 [5120, 512], P('fsdp')
The draws below stay inside these ranges and needn't reach their ends.
All inputs are finite; a program needn't handle non-finite values.
Results may differ from the reference program's by a relative error of at most 0.001.
Values may be sent and summed in bfloat16 or wider, within the bound.
No kernel may reach another device: no remote copies, remote signals or barrier semaphores. Data moves between devices by JAX's collectives and lax.ppermute only.
A program may use at most 256 MiB of HBM per device.

```python
import jax
import jax.numpy as jnp
from jax import lax

D = 5120
KV = 512
SPAN = 64
KEEP = 8
TOK_DEV = 1024
TOKENS = 131072
N_REP = 64
N_FSDP = 2


def spiked(array, stream_key, source, target, parts, factor):
    def block_of(position):
        return (jnp.arange(array.shape[position]) // (array.shape[position] // parts)).reshape((-1,) + (1,) * (array.ndim - 1 - position))

    one_side = jax.random.permutation(stream_key, parts)[block_of(target)]
    second = (block_of(target) + parts // 2) % parts
    return jnp.where((block_of(source) == one_side) | (block_of(source) == second), factor * array, array)


def shard_levels(rng, shape, shards, smallest, top_value):
    gain, own = 1.0, jax.random.fold_in(rng, 6)
    for dim, blocks in shards:
        draws = jnp.exp(jax.random.uniform(jax.random.fold_in(own, dim), (blocks,), jnp.float32, smallest / len(shards), top_value / len(shards)))
        gain = gain * jnp.repeat(draws, shape[dim] // blocks).reshape([-1 if axis == dim else 1 for axis in range(len(shape))])
    return gain


def normal_values(rng, shape, deviation, limit, split=(), kind=jnp.bfloat16):
    entries = jax.random.normal(rng, shape, jnp.float32) * deviation
    if len(split) > 0:
        entries = shard_levels(rng, shape, split, -0.22, 0.18) * entries
    return jnp.clip(entries, min=-limit, max=limit).astype(kind)


def bell_draw_with(own_key, shape, width, most, pieces, heavy, kind=jnp.bfloat16):
    array = width * jax.random.normal(own_key, shape, jnp.float32)
    if pieces:
        array = array * shard_levels(own_key, shape, pieces, -0.22, 0.18)
    return jnp.clip(spiked(array, jax.random.fold_in(own_key, 3), *heavy), -most, most).astype(kind)


def setup_inputs(seed: int = 0) -> dict:
    seeds = jax.random.split(jax.random.key(seed), 5)
    acts = bell_draw_with(seeds[0], (TOKENS, D), 1.0, 24.0, ((0, 128),), (0, 1, 128, 5.5))
    cotangent = normal_values(seeds[1], (TOKENS, KV), (TOK_DEV * N_FSDP) ** -0.5, 0.125, ((0, 128),))
    weight = normal_values(seeds[2], (D, KV), D ** -0.5, 0.078125, ((0, 2),))
    momentum = normal_values(seeds[3], (N_REP, D, KV), 1.0, 6.0, ((0, 64), (1, 2)), jnp.float32)
    return dict(acts=acts, cotangent=cotangent, weight=weight, momentum=momentum)


BETA = 0.9
RATE = 0.02

def dct_rows():
    freq = jnp.arange(KEEP)[:, None].astype(jnp.float32)
    cell = jnp.arange(SPAN)[None, :].astype(jnp.float32)
    scale = jnp.where(freq == 0, jnp.sqrt(1.0 / SPAN), jnp.sqrt(2.0 / SPAN)).astype(jnp.float32)
    return (scale * jnp.cos(jnp.pi * (2.0 * cell + 1.0) * freq / (2.0 * SPAN))).astype(jnp.float32)

def encode(field, basis):
    blocks = field.reshape(D // SPAN, SPAN, KV // SPAN, SPAN)
    return jnp.einsum('kn,anbm,lm->akbl', basis, blocks, basis, precision=lax.Precision.HIGHEST)

def decode(coeffs, basis):
    blocks = jnp.einsum('kn,akbl,lm->anbm', basis, coeffs, basis, precision=lax.Precision.HIGHEST)
    return blocks.reshape(D, KV)

def reference(acts, cotangent, weight, momentum):
    basis = dct_rows()
    group = TOK_DEV * N_FSDP

    def one_replica(index):
        start = (index * group).astype(jnp.int32)
        inputs = lax.dynamic_slice_in_dim(acts, start, group, 0).astype(jnp.float32)
        grads_out = lax.dynamic_slice_in_dim(cotangent, start, group, 0).astype(jnp.float32)
        grad = jnp.dot(inputs.T, grads_out, precision=lax.Precision.HIGHEST)
        fresh = BETA * momentum[index] + grad
        coeffs = encode(fresh, basis)
        return (fresh - decode(coeffs, basis), coeffs)
    new_momentum, coeffs = lax.map(one_replica, jnp.arange(N_REP, dtype=jnp.int32))
    total = lax.optimization_barrier(jnp.sum(coeffs, axis=0))
    update = decode(total, basis)
    new_weight = (weight.astype(jnp.float32) - RATE * update).astype(jnp.bfloat16)
    return (new_momentum, update, new_weight)
```

```python
import jax
import jax.numpy as jnp
import ml_dtypes
import numpy as np
from jax import lax
from jax.experimental import pallas as pl
from jax.experimental.pallas import tpu as pltpu
from jax.sharding import PartitionSpec as P

SPAN = 64
KEEP = 8
BETA = 0.9
RATE = 0.02

TOK = 1024
KV = 512
HALF = 2560
STEP = 512
STEPS = HALF // STEP
BANDS = KV // SPAN * KEEP
GROUP = STEP // SPAN * KEEP

BF = jnp.bfloat16
F32 = jnp.float32


def dct_rows():
    freq = np.arange(KEEP)[:, None].astype(np.float64)
    cell = np.arange(SPAN)[None, :].astype(np.float64)
    scale = np.where(freq == 0, np.sqrt(1.0 / SPAN), np.sqrt(2.0 / SPAN))
    return (scale * np.cos(np.pi * (2.0 * cell + 1.0) * freq / (2.0 * SPAN))).astype(np.float32)


def terms(array):
    out, rest = [], array.astype(np.float32)
    for _ in range(3):
        part = rest.astype(ml_dtypes.bfloat16)
        out.append(part)
        rest = rest - part.astype(np.float32)
    return out


def basis_terms():
    return terms(np.kron(np.eye(STEP // SPAN, dtype=np.float32), dct_rows()))


def encoder_rows():
    return np.concatenate(basis_terms(), axis=0)


def encoder_cols():
    return np.concatenate([t.T for t in basis_terms()], axis=1)


PAIRS = ((0, 0), (0, 1), (1, 0), (0, 2), (2, 0), (1, 1))


def decoder_cols():
    t = basis_terms()
    return np.concatenate([t[j] for _, j in PAIRS], axis=0)


def decoder_rows():
    t = basis_terms()
    return np.concatenate([t[i].T for i, _ in PAIRS], axis=1)


def split(x):
    hi = x.astype(BF)
    rest = x - hi.astype(F32)
    mid = rest.astype(BF)
    lo = (rest - mid.astype(F32)).astype(BF)
    return hi, mid, lo


def dot(a, b, dims=((1,), (0,))):
    return lax.dot_general(a, b, (dims, ((), ())), preferred_element_type=F32)


def cross(product, rows, cols):
    total = None
    for i, j in reversed(PAIRS):
        piece = product[i * rows : (i + 1) * rows, j * cols : (j + 1) * cols]
        total = piece if total is None else total + piece
    return total


def encode_tokens(cot_ref, enc_rows_ref, z_ref):
    z = dot(enc_rows_ref[...], cot_ref[...], ((1,), (1,)))
    z = z[2 * BANDS :] + z[BANDS : 2 * BANDS] + z[:BANDS]
    hi, mid, lo = split(z)
    z_ref[:BANDS] = hi
    z_ref[BANDS : 2 * BANDS] = mid
    z_ref[2 * BANDS :] = lo


def encode_step(acts_ref, z_ref, enc_cols_ref):
    g = dot(z_ref[...], acts_ref[...])
    g = g[2 * BANDS :] + g[BANDS : 2 * BANDS] + g[:BANDS]
    return cross(dot(jnp.concatenate(split(g), axis=0), enc_cols_ref[...]), BANDS, GROUP)


def assemble(held_ref, out_ref):
    out_ref[...] = jnp.concatenate([held_ref[i] for i in range(STEPS)], axis=1)


def coeffs_kernel(which, cot_ref, enc_rows_ref, enc_cols_ref, acts_ref, out_ref, z_ref, held_ref):
    step = pl.program_id(0)

    @pl.when(step == 0)
    def _():
        encode_tokens(cot_ref, enc_rows_ref, z_ref)

    held_ref[step] = encode_step(acts_ref, z_ref, enc_cols_ref)

    @pl.when(step == STEPS - 1)
    def _():
        assemble(held_ref, out_ref)


def coeffs_momentum_kernel(
    which, cot_ref, enc_rows_ref, enc_cols_ref, acts_ref, mom_ref, out_ref, z_ref, held_ref
):
    step = pl.program_id(0)

    @pl.when(step == 0)
    def _():
        encode_tokens(cot_ref, enc_rows_ref, z_ref)

    hi, mid, lo = split(mom_ref[0])
    rows = GROUP
    enc = enc_rows_ref[...]
    a = dot(enc, hi)
    b = dot(enc[: 2 * rows], mid)
    c = dot(enc[:rows], lo)
    t = (c + b[rows:] + a[2 * rows :]) + (b[:rows] + a[rows : 2 * rows]) + a[:rows]
    e = cross(dot(jnp.concatenate(split(t), axis=0), enc_cols_ref[...]), GROUP, BANDS)
    held_ref[step] = encode_step(acts_ref, z_ref, enc_cols_ref) + BETA * e.T

    @pl.when(step == STEPS - 1)
    def _():
        assemble(held_ref, out_ref)


def gradient_kernel(which, cot_ref, acts_ref, out_ref):
    out_ref[...] = dot(acts_ref[...], cot_ref[...], ((0,), (0,)))


def decode_step(coeffs, dec_cols_ref, dec_rows_ref):
    t = split(coeffs)
    wide = dot(jnp.concatenate([t[i] for i, _ in PAIRS], axis=1), dec_cols_ref[...])
    w = split(wide)
    return dot(dec_rows_ref[...], jnp.concatenate([w[j] for _, j in PAIRS], axis=0))


def momentum_kernel(
    which, cot_ref, dec_cols_ref, dec_rows_ref, coeffs_ref, acts_ref, mom_ref, recv_ref, out_ref
):
    g = dot(acts_ref[...], cot_ref[...], ((0,), (0,)))
    fresh = BETA * mom_ref[0] + (g + recv_ref[...])
    out_ref[0] = fresh - decode_step(coeffs_ref[0], dec_cols_ref, dec_rows_ref)


def update_kernel(dec_cols_ref, dec_rows_ref, coeffs_ref, weight_ref, update_ref, new_ref):
    update = decode_step(coeffs_ref[0], dec_cols_ref, dec_rows_ref)
    update_ref[...] = update
    new_ref[...] = (weight_ref[...].astype(F32) - RATE * update).astype(BF)


def whole(shape):
    return pl.BlockSpec(shape, lambda *_: (0,) * len(shape))


def params():
    return pltpu.CompilerParams(vmem_limit_bytes=48 * 1024 * 1024)


def half_call(kernel, which, fixed, streamed, specs, out_spec, out_shape, scratch, flops, nbytes):
    return pl.pallas_call(
        kernel,
        grid_spec=pltpu.PrefetchScalarGridSpec(
            num_scalar_prefetch=1,
            grid=(STEPS,),
            in_specs=[whole(a.shape) for a in fixed] + specs,
            out_specs=out_spec,
            scratch_shapes=scratch,
        ),
        out_shape=out_shape,
        compiler_params=params(),
        cost_estimate=pl.CostEstimate(flops=flops, bytes_accessed=nbytes, transcendentals=0),
    )(which, *fixed, *streamed)


ACTS = pl.BlockSpec((TOK, STEP), lambda i, s: (0, s[0] * STEPS + i))
MOM = pl.BlockSpec((1, STEP, KV), lambda i, s: (0, i, 0))
ROWS = pl.BlockSpec((STEP, KV), lambda i, s: (i, 0))
COEFF_SCRATCH = lambda: [pltpu.VMEM((3 * BANDS, TOK), BF), pltpu.VMEM((STEPS, BANDS, GROUP), F32)]


def per_step(coeffs):
    return coeffs.reshape(BANDS, STEPS, GROUP).transpose(1, 2, 0)


def shift(axis, by):
    pairs = []
    for z in range(4):
        for y in range(4):
            for x in range(4):
                to = [z, y, x]
                to[axis] = (to[axis] + by) % 4
                pairs.append((z * 16 + y * 4 + x, to[0] * 16 + to[1] * 4 + to[2]))
    return pairs


def sum_replicas(x):
    for axis in (2, 1, 0):
        a, b, c = (lax.ppermute(x, "rep", shift(axis, by)) for by in (1, 3, 2))
        x = (x + c) + (a + b)
    return x


SWAP = ((0, 1), (1, 0))


def shards(acts, cotangent, weight, momentum):
    core = lax.axis_index("fsdp").astype(jnp.int32)
    own, other = core.reshape(1), (1 - core).reshape(1)
    enc_rows, enc_cols = jnp.asarray(encoder_rows()), jnp.asarray(encoder_cols())
    dec_cols, dec_rows = jnp.asarray(decoder_cols()), jnp.asarray(decoder_rows())
    shape = jax.ShapeDtypeStruct((BANDS, STEPS * GROUP), F32)

    theirs = half_call(
        coeffs_kernel, other, [cotangent, enc_rows, enc_cols], [acts], [ACTS],
        whole(shape.shape), shape, COEFF_SCRATCH(), 2 * TOK * HALF * 192, 6_500_000,
    )
    got = lax.ppermute(theirs, "fsdp", SWAP)
    mine = half_call(
        coeffs_momentum_kernel, own, [cotangent, enc_rows, enc_cols], [acts, momentum], [ACTS, MOM],
        whole(shape.shape), shape, COEFF_SCRATCH(), 2 * TOK * HALF * 300, 12_000_000,
    )
    coeffs = mine + got
    total = sum_replicas(coeffs)

    partial = half_call(
        gradient_kernel, other, [cotangent], [acts], [ACTS],
        ROWS, jax.ShapeDtypeStruct((HALF, KV), F32), [], 2 * TOK * HALF * KV, 12_000_000,
    )
    received = lax.ppermute(partial, "fsdp", SWAP)
    coeff_spec = pl.BlockSpec((1, GROUP, BANDS), lambda i, s: (i, 0, 0))
    new_momentum = half_call(
        momentum_kernel, own, [cotangent, dec_cols, dec_rows], [per_step(coeffs), acts, momentum, received],
        [coeff_spec, ACTS, MOM, ROWS], MOM, jax.ShapeDtypeStruct((1, HALF, KV), F32), [],
        2 * TOK * HALF * 700, 23_000_000,
    )

    rows = pl.BlockSpec((STEP, KV), lambda i: (i, 0))
    update, new_weight = pl.pallas_call(
        update_kernel,
        grid=(STEPS,),
        in_specs=[
            whole(dec_cols.shape), whole(dec_rows.shape),
            pl.BlockSpec((1, GROUP, BANDS), lambda i: (i, 0, 0)), rows,
        ],
        out_specs=[rows, rows],
        out_shape=[jax.ShapeDtypeStruct((HALF, KV), F32), jax.ShapeDtypeStruct((HALF, KV), BF)],
        compiler_params=params(),
        cost_estimate=pl.CostEstimate(flops=2 * HALF * KV * 400, bytes_accessed=11_000_000, transcendentals=0),
    )(dec_cols, dec_rows, per_step(total), weight)
    return new_momentum, update, new_weight


def solution(mesh):
    in_specs = (
        P(("rep", "fsdp"), None),
        P(("rep", "fsdp"), None),
        P("fsdp", None),
        P("rep", "fsdp", None),
    )
    out_specs = (P("rep", "fsdp", None), P("fsdp", None), P("fsdp", None))
    return jax.shard_map(shards, mesh=mesh, in_specs=in_specs, out_specs=out_specs, check_vma=False)
```

```python
import jax
import jax.numpy as jnp
import ml_dtypes
import numpy as np
from jax import lax
from jax.experimental import pallas as pl
from jax.experimental.pallas import tpu as pltpu
from jax.sharding import PartitionSpec as P

SPAN = 64
KEEP = 8
BETA = 0.9
RATE = 0.02

TOK = 1024
KV = 512
HALF = 2560
UNIT = 256
KEPT = UNIT // SPAN * KEEP
BANDS = KV // SPAN * KEEP
ROWS_KEPT = HALF // SPAN * KEEP

WIDE = 1280
STEPS = HALF // WIDE
MOM_STEP = 512
UPD_STEP = 512
VMEM_LIMIT = 24 * 1024 * 1024

BF = jnp.bfloat16
F32 = jnp.float32


def dct_rows():
    freq = np.arange(KEEP)[:, None].astype(np.float64)
    cell = np.arange(SPAN)[None, :].astype(np.float64)
    scale = np.where(freq == 0, np.sqrt(1.0 / SPAN), np.sqrt(2.0 / SPAN))
    return (scale * np.cos(np.pi * (2.0 * cell + 1.0) * freq / (2.0 * SPAN))).astype(np.float32)


def basis_terms(size):
    out, rest = [], np.kron(np.eye(size // SPAN, dtype=np.float32), dct_rows())
    for _ in range(3):
        part = rest.astype(ml_dtypes.bfloat16)
        out.append(part)
        rest = rest - part.astype(np.float32)
    return out


PAIRS = ((0, 0), (0, 1), (1, 0), (1, 1), (0, 2), (2, 0))


def encoder_rows(size):
    return jnp.asarray(np.concatenate(basis_terms(size), axis=0))


def encoder_cols(size):
    return jnp.asarray(np.concatenate([t.T for t in basis_terms(size)], axis=1))


def decoder_cols(pairs):
    t = basis_terms(KV)
    return jnp.asarray(np.concatenate([t[j] for _, j in pairs], axis=0))


def decoder_rows(pairs):
    t = basis_terms(UNIT)
    return jnp.asarray(np.concatenate([t[i].T for i, _ in pairs], axis=1))


def split(x):
    hi = x.astype(BF)
    rest = x - hi.astype(F32)
    mid = rest.astype(BF)
    lo = (rest - mid.astype(F32)).astype(BF)
    return hi, mid, lo


def dot(a, b, dims=((1,), (0,))):
    return lax.dot_general(a, b, (dims, ((), ())), preferred_element_type=F32)


def cross(product, rows, cols):
    total = None
    for i, j in reversed(PAIRS):
        piece = product[i * rows : (i + 1) * rows, j * cols : (j + 1) * cols]
        total = piece if total is None else total + piece
    return total


def copies_of(pairs, sems):
    made = [pltpu.make_async_copy(source, target, sems.at[k]) for k, (source, target) in enumerate(pairs)]
    for copy in made:
        copy.start()
    return made


def encode_chunk(g, enc_cols):
    t = split(g)
    pieces = []
    for k in range(WIDE // UNIT):
        stacked = jnp.concatenate([x[:, k * UNIT : (k + 1) * UNIT] for x in t], axis=0)
        pieces.append(cross(dot(stacked, enc_cols), BANDS, KEPT))
    return jnp.concatenate(pieces, axis=1)


def tokens_kernel(
    order, cot_hbm, enc_kv_hbm, enc_cols_hbm, acts_hbm,
    theirs_ref, mine_ref, cot_ref, acts_theirs_ref, acts_mine_ref, enc_kv_ref, enc_cols_ref, z_ref, sems,
):
    chunks = [(half, c) for half in range(2) for c in range(STEPS)]
    targets = (acts_theirs_ref, acts_mine_ref)
    pairs = [(enc_kv_hbm, enc_kv_ref), (cot_hbm, cot_ref)]
    for half, c in chunks:
        start = pl.multiple_of(order[half] * HALF + c * WIDE, WIDE)
        pairs.append((acts_hbm.at[:, pl.ds(start, WIDE)], targets[half].at[:, pl.ds(c * WIDE, WIDE)]))
    pairs.append((enc_cols_hbm, enc_cols_ref))
    copies = copies_of(pairs, sems)
    copies[0].wait()
    copies[1].wait()

    z = dot(enc_kv_ref[...], cot_ref[...], ((1,), (1,)))
    z_ref[...] = jnp.concatenate(split(z[2 * BANDS :] + z[BANDS : 2 * BANDS] + z[:BANDS]), axis=0)
    copies[-1].wait()

    found, before = [], None
    for k, (half, c) in enumerate(chunks):
        copies[2 + k].wait()
        g = dot(z_ref[...], targets[half][:, c * WIDE : (c + 1) * WIDE])
        if before is not None:
            found.append(encode_chunk(before, enc_cols_ref[...]))
        before = g[2 * BANDS :] + g[BANDS : 2 * BANDS] + g[:BANDS]
    found.append(encode_chunk(before, enc_cols_ref[...]))
    theirs_ref[...] = jnp.concatenate(found[:STEPS], axis=1)
    mine_ref[...] = jnp.concatenate(found[STEPS:], axis=1)


def momentum_coeffs_kernel(enc_rows_ref, enc_cols_ref, mine_ref, mom_hbm, out_ref, mom_ref, sems):
    steps = HALF // MOM_STEP
    copies = copies_of([(mom_hbm.at[0, pl.ds(k * MOM_STEP, MOM_STEP)], mom_ref.at[pl.ds(k * MOM_STEP, MOM_STEP)]) for k in range(steps)], sems)
    enc = enc_rows_ref[...]
    found = []
    for step in range(steps):
        copies[step].wait()
        for k in range(MOM_STEP // UNIT):
            start = step * MOM_STEP + k * UNIT
            hi, mid, lo = split(mom_ref[start : start + UNIT])
            a = dot(enc, hi)
            b = dot(enc[: 2 * KEPT], mid)
            c = dot(enc[:KEPT], lo)
            t = (c + b[KEPT:] + a[2 * KEPT :]) + (b[:KEPT] + a[KEPT : 2 * KEPT]) + a[:KEPT]
            found.append(cross(dot(jnp.concatenate(split(t), axis=0), enc_cols_ref[...]), KEPT, BANDS))
    out_ref[...] = mine_ref[...] + BETA * jnp.concatenate(found, axis=0).T


def gradient_kernel(dep, cot_ref, acts_ref, out_ref):
    for k in range(HALF // MOM_STEP):
        rows = slice(k * MOM_STEP, (k + 1) * MOM_STEP)
        out_ref[rows] = dot(acts_ref[:, rows], cot_ref[...], ((0,), (0,)))


def decode_cols(coeffs, dec_cols_ref, out_ref, pairs):
    t = split(coeffs)
    wide = dot(jnp.concatenate([t[i] for i, _ in pairs], axis=0), dec_cols_ref[...], ((0,), (0,)))
    w = split(wide)
    for g in range(HALF // UNIT):
        out_ref[g] = jnp.concatenate([w[j][g * KEPT : (g + 1) * KEPT] for _, j in pairs], axis=0)


def momentum_kernel(
    dec_cols_ref, dec_rows_ref, coeffs_ref, cot_ref, acts_ref, mom_ref, recv_ref, out_hbm, wide_ref, out_ref, sems
):
    decode_cols(coeffs_ref[...], dec_cols_ref, wide_ref, PAIRS)
    copies = []
    for step in range(HALF // MOM_STEP):
        for k in range(MOM_STEP // UNIT):
            start = step * MOM_STEP + k * UNIT
            rows = slice(start, start + UNIT)
            g = dot(acts_ref[:, rows], cot_ref[...], ((0,), (0,)))
            fresh = BETA * mom_ref[rows] + (g + recv_ref[rows])
            out_ref[rows] = fresh - dot(dec_rows_ref[...], wide_ref[start // UNIT])
        rows = pl.ds(step * MOM_STEP, MOM_STEP)
        copy = pltpu.make_async_copy(out_ref.at[rows], out_hbm.at[0, rows], sems.at[step])
        copy.start()
        copies.append(copy)
    for copy in copies:
        copy.wait()


def update_kernel(dec_cols_ref, dec_rows_ref, coeffs_ref, weight_ref, update_ref, new_ref, wide_ref):
    step = pl.program_id(0)

    @pl.when(step == 0)
    def _():
        decode_cols(coeffs_ref[...], dec_cols_ref, wide_ref, PAIRS[:3])

    for k in range(UPD_STEP // UNIT):
        rows = slice(k * UNIT, (k + 1) * UNIT)
        update = dot(dec_rows_ref[...], wide_ref[step * (UPD_STEP // UNIT) + k])
        update_ref[rows] = update
        new_ref[rows] = (weight_ref[rows].astype(F32) - RATE * update).astype(BF)


def whole(array):
    return pl.BlockSpec(array.shape, lambda *_: (0,) * len(array.shape))


def held(shape, dtype=F32):
    return pltpu.VMEM(shape, dtype)


def in_hbm(array):
    return pltpu.with_memory_space_constraint(array, pltpu.HBM)


def in_vmem(array):
    return pltpu.with_memory_space_constraint(array, pltpu.VMEM)


ANY = pl.BlockSpec(memory_space=pl.ANY)
INSIDE = pl.BlockSpec(memory_space=pltpu.VMEM)


def single(kernel, operands, specs, out_specs, out_shape, scratch, flops, nbytes):
    return pl.pallas_call(
        kernel,
        in_specs=specs,
        out_specs=out_specs,
        out_shape=out_shape,
        scratch_shapes=scratch,
        compiler_params=pltpu.CompilerParams(vmem_limit_bytes=VMEM_LIMIT),
        cost_estimate=pl.CostEstimate(flops=flops, bytes_accessed=nbytes, transcendentals=0),
    )(*operands)


def call(kernel, steps, scalars, fixed, streamed, specs, out_specs, out_shape, scratch, flops, nbytes):
    return pl.pallas_call(
        kernel,
        grid_spec=pltpu.PrefetchScalarGridSpec(
            num_scalar_prefetch=len(scalars),
            grid=(steps,),
            in_specs=[whole(a) for a in fixed] + specs,
            out_specs=out_specs,
            scratch_shapes=scratch,
        ),
        out_shape=out_shape,
        compiler_params=pltpu.CompilerParams(vmem_limit_bytes=VMEM_LIMIT),
        cost_estimate=pl.CostEstimate(flops=flops, bytes_accessed=nbytes, transcendentals=0),
    )(*scalars, *fixed, *streamed)


COEFFS = jax.ShapeDtypeStruct((BANDS, ROWS_KEPT), F32)


def shift(axis, by):
    pairs = []
    for z in range(4):
        for y in range(4):
            for x in range(4):
                to = [z, y, x]
                to[axis] = (to[axis] + by) % 4
                pairs.append((z * 16 + y * 4 + x, to[0] * 16 + to[1] * 4 + to[2]))
    return pairs


def sum_axis(x, axis):
    a, b, c = (lax.ppermute(x, "rep", shift(axis, by)) for by in (1, 3, 2))
    return (x + c) + (a + b)


SWAP = ((0, 1), (1, 0))


def shards(acts, cotangent, weight, momentum):
    core = lax.axis_index("fsdp").astype(jnp.int32)
    enc_kv, enc_kv_cols = encoder_rows(KV), encoder_cols(KV)
    enc_rows, enc_cols = encoder_rows(UNIT), encoder_cols(UNIT)
    half = (HALF, KV)

    theirs, mine, cot, acts_theirs, acts_mine = single(
        tokens_kernel,
        [jnp.stack([1 - core, core]), *map(in_hbm, (cotangent, enc_kv, enc_cols, acts))],
        [pl.BlockSpec(memory_space=pltpu.SMEM)] + [ANY] * 4,
        [INSIDE] * 5,
        [COEFFS, COEFFS, held((TOK, KV), BF), held((TOK, HALF), BF), held((TOK, HALF), BF)],
        [held(enc_kv.shape, BF), held(enc_cols.shape, BF), held((3 * BANDS, TOK), BF), pltpu.SemaphoreType.DMA((7,))],
        2 * TOK * 2 * HALF * 192, 12_000_000,
    )
    got = lax.ppermute(theirs, "fsdp", SWAP)
    mine, mom = single(
        momentum_coeffs_kernel, [enc_rows, enc_kv_cols, mine, in_hbm(momentum)], [INSIDE] * 3 + [ANY],
        [INSIDE] * 2, [COEFFS, held(half)], [pltpu.SemaphoreType.DMA((HALF // MOM_STEP,))],
        2 * HALF * KV * 192, 6_000_000,
    )
    coeffs = mine + got

    partial = single(
        gradient_kernel, [coeffs, in_vmem(cot), in_vmem(acts_theirs)], [ANY, INSIDE, INSIDE],
        INSIDE, held(half), [], 2 * TOK * HALF * KV, 12_000_000,
    )
    total, partial = lax.optimization_barrier((sum_axis(coeffs, 2), partial))
    received = lax.ppermute(partial, "fsdp", SWAP)
    total, coeffs, received = lax.optimization_barrier((sum_axis(total, 1), coeffs, received))
    new_momentum = single(
        momentum_kernel,
        [decoder_cols(PAIRS), decoder_rows(PAIRS), coeffs, *map(in_vmem, (cot, acts_mine, mom, received))],
        [INSIDE] * 7, ANY, jax.ShapeDtypeStruct((1, HALF, KV), F32),
        [held((HALF // UNIT, 6 * KEPT, KV), BF), held(half), pltpu.SemaphoreType.DMA((HALF // MOM_STEP,))],
        2 * TOK * HALF * 700, 23_000_000,
    )
    total, new_momentum = lax.optimization_barrier((sum_axis(total, 0), new_momentum))

    rows = pl.BlockSpec((UPD_STEP, KV), lambda i: (i, 0))
    update, new_weight = call(
        update_kernel, HALF // UPD_STEP, [], [decoder_cols(PAIRS[:3]), decoder_rows(PAIRS[:3]), total],
        [weight], [rows], [rows, rows],
        [jax.ShapeDtypeStruct((HALF, KV), F32), jax.ShapeDtypeStruct((HALF, KV), BF)],
        [pltpu.VMEM((HALF // UNIT, 3 * KEPT, KV), BF)], 2 * HALF * KV * 400, 11_000_000,
    )
    return new_momentum, update, new_weight


def solution(mesh):
    in_specs = (
        P(("rep", "fsdp"), None),
        P(("rep", "fsdp"), None),
        P("fsdp", None),
        P("rep", "fsdp", None),
    )
    out_specs = (P("rep", "fsdp", None), P("fsdp", None), P("fsdp", None))
    return jax.shard_map(shards, mesh=mesh, in_specs=in_specs, out_specs=out_specs, check_vma=False)
```

```python
import jax
import jax.numpy as jnp
import ml_dtypes
import numpy as np
from jax import lax
from jax.experimental import pallas as pl
from jax.experimental.pallas import tpu as pltpu
from jax.sharding import PartitionSpec as P

SPAN = 64
KEEP = 8
BETA = 0.9
RATE = 0.02

TOK = 1024
KV = 512
HALF = 2560
UNIT = 256
KEPT = UNIT // SPAN * KEEP
BANDS = KV // SPAN * KEEP
ROWS_KEPT = HALF // SPAN * KEEP

THEIRS_CHUNKS = ((0, 512), (512, 1024), (1024, 1536), (1536, 2048), (2048, 2560))
MINE_CHUNKS = ((0, 1024), (1024, 2048), (2048, 2560))
MINE_ORDER = (("m", 0), ("a", 0), ("m", 1), ("m", 2), ("a", 1), ("m", 3), ("m", 4), ("a", 2))
MOM_STEP = 512
FIRST = 1536
VMEM_LIMIT = 24 * 1024 * 1024

BF = jnp.bfloat16
F32 = jnp.float32


def dct_rows():
    freq = np.arange(KEEP)[:, None].astype(np.float64)
    cell = np.arange(SPAN)[None, :].astype(np.float64)
    scale = np.where(freq == 0, np.sqrt(1.0 / SPAN), np.sqrt(2.0 / SPAN))
    return (scale * np.cos(np.pi * (2.0 * cell + 1.0) * freq / (2.0 * SPAN))).astype(np.float32)


def basis_terms(size):
    out, rest = [], np.kron(np.eye(size // SPAN, dtype=np.float32), dct_rows())
    for _ in range(3):
        part = rest.astype(ml_dtypes.bfloat16)
        out.append(part)
        rest = rest - part.astype(np.float32)
    return out


PAIRS = ((0, 0), (0, 1), (1, 0), (1, 1), (0, 2), (2, 0))


def encoder_rows(size):
    return jnp.asarray(np.concatenate(basis_terms(size), axis=0))


def encoder_cols(size):
    return jnp.asarray(np.concatenate([t.T for t in basis_terms(size)], axis=1))


def decoder_cols(pairs):
    t = basis_terms(KV)
    return jnp.asarray(np.concatenate([t[j] for _, j in pairs], axis=0))


def decoder_rows(pairs):
    t = basis_terms(UNIT)
    return jnp.asarray(np.concatenate([t[i].T for i, _ in pairs], axis=1))


def split(x):
    hi = x.astype(BF)
    rest = x - hi.astype(F32)
    mid = rest.astype(BF)
    lo = (rest - mid.astype(F32)).astype(BF)
    return hi, mid, lo


def dot(a, b, dims=((1,), (0,))):
    return lax.dot_general(a, b, (dims, ((), ())), preferred_element_type=F32)


def cross(product, rows, cols):
    total = None
    for i, j in reversed(PAIRS):
        piece = product[i * rows : (i + 1) * rows, j * cols : (j + 1) * cols]
        total = piece if total is None else total + piece
    return total


class Arrivals:
    def __init__(self, pairs, sems, ahead):
        self.copies = [pltpu.make_async_copy(a, b, sems.at[k]) for k, (a, b) in enumerate(pairs)]
        self.started, self.waited, self.ahead = 0, 0, ahead
        self.fill()

    def fill(self):
        while self.started < min(len(self.copies), self.waited + self.ahead):
            self.copies[self.started].start()
            self.started += 1

    def next(self):
        self.copies[self.waited].wait()
        self.waited += 1
        self.fill()


def encode_chunk(g, enc_cols):
    t = split(g)
    pieces = []
    for k in range(g.shape[1] // UNIT):
        stacked = jnp.concatenate([x[:, k * UNIT : (k + 1) * UNIT] for x in t], axis=0)
        pieces.append(cross(dot(stacked, enc_cols), BANDS, KEPT))
    return pieces


def acts_copies(acts_hbm, acts_ref, half, chunks):
    pairs = []
    for lo, hi in chunks:
        start = pl.multiple_of(half * HALF + lo, UNIT)
        pairs.append((acts_hbm.at[:, pl.ds(start, hi - lo)], acts_ref.at[:, lo:hi]))
    return pairs


def encode_acts(z_ref, acts_ref, lo, hi):
    g = dot(z_ref[...], acts_ref[:, lo:hi])
    return g[BANDS:] + g[:BANDS]


def theirs_kernel(
    half, cot_hbm, enc_kv_hbm, enc_cols_hbm, acts_hbm,
    theirs_ref, cot_ref, z_ref, acts_ref, enc_kv_ref, enc_cols_ref, sems,
):
    pairs = [(enc_kv_hbm, enc_kv_ref), (cot_hbm, cot_ref), (enc_cols_hbm, enc_cols_ref)]
    pairs += acts_copies(acts_hbm, acts_ref, half[0], THEIRS_CHUNKS)
    arrivals = Arrivals(pairs, sems, 5)
    arrivals.next()
    arrivals.next()

    z = dot(enc_kv_ref[...], cot_ref[...], ((1,), (1,)))
    z_ref[...] = jnp.concatenate(split(z[2 * BANDS :] + z[BANDS : 2 * BANDS] + z[:BANDS])[:2], axis=0)
    arrivals.next()

    found, before = [], None
    for lo, hi in THEIRS_CHUNKS:
        arrivals.next()
        g = encode_acts(z_ref, acts_ref, lo, hi)
        if before is not None:
            found += encode_chunk(before, enc_cols_ref[...])
        before = g
    found += encode_chunk(before, enc_cols_ref[...])
    theirs_ref[...] = jnp.concatenate(found, axis=1)


def mine_kernel(
    half, z_ref, enc_rows_ref, enc_kv_cols_ref, enc_cols_ref, acts_hbm, mom_hbm,
    mine_ref, acts_ref, mom_ref, sems,
):
    from_acts = acts_copies(acts_hbm, acts_ref, half[0], MINE_CHUNKS)
    rows = [pl.ds(k * MOM_STEP, MOM_STEP) for k in range(HALF // MOM_STEP)]
    from_mom = [(mom_hbm.at[0, r], mom_ref.at[r]) for r in rows]
    arrivals = Arrivals([(from_acts if kind == "a" else from_mom)[k] for kind, k in MINE_ORDER], sems, 3)
    enc = enc_rows_ref[...]

    def encode_rows(start):
        m = mom_ref[start : start + UNIT]
        hi = m.astype(BF)
        a = dot(enc, hi)
        b = dot(enc[: 2 * KEPT], (m - hi.astype(F32)).astype(BF))
        return (b[KEPT:] + a[2 * KEPT :]) + (b[:KEPT] + a[KEPT : 2 * KEPT]) + a[:KEPT]

    def encode_cols(parts):
        n = len(parts) * KEPT
        terms = split(jnp.concatenate(parts, axis=0))
        return cross(dot(jnp.concatenate(terms, axis=0), enc_kv_cols_ref[...]), n, BANDS)

    found, from_rows, before = [], [], None
    for kind, k in MINE_ORDER + ((None, 0),):
        done = before
        if kind is not None:
            arrivals.next()
            if kind == "a":
                before = kind, encode_acts(z_ref, acts_ref, *MINE_CHUNKS[k])
            else:
                before = kind, [encode_rows(k * MOM_STEP + i * UNIT) for i in range(MOM_STEP // UNIT)]
        if done is not None:
            if done[0] == "a":
                found += encode_chunk(done[1], enc_cols_ref[...])
            else:
                from_rows.append(encode_cols(done[1]))
    mine_ref[...] = jnp.concatenate(found, axis=1) + BETA * jnp.concatenate(from_rows, axis=0).T


def gradient_kernel(dep, cot_ref, acts_ref, out_ref):
    for k in range(HALF // MOM_STEP):
        rows = slice(k * MOM_STEP, (k + 1) * MOM_STEP)
        out_ref[rows] = dot(acts_ref[:, rows], cot_ref[...], ((0,), (0,)))


def decode_cols(coeffs, dec_cols_ref, out_ref, pairs):
    t = split(coeffs)
    wide = dot(jnp.concatenate([t[i] for i, _ in pairs], axis=0), dec_cols_ref[...], ((0,), (0,)))
    w = split(wide)
    for g in range(HALF // UNIT):
        out_ref[g] = jnp.concatenate([w[j][g * KEPT : (g + 1) * KEPT] for _, j in pairs], axis=0)


def own_rows(start, dec_rows_ref, wide, cot_ref, acts_ref, mom_ref):
    rows = slice(start, start + UNIT)
    g = dot(acts_ref[:, rows], cot_ref[...], ((0,), (0,)))
    return BETA * mom_ref[rows] + g - dot(dec_rows_ref[...], wide)


def first_rows_kernel(
    dep, dec_cols_ref, dec_rows_ref, coeffs_ref, cot_ref, acts_ref, mom_ref, out_ref, wide_ref
):
    decode_cols(coeffs_ref[...], dec_cols_ref, wide_ref, PAIRS)
    for start in range(0, FIRST, UNIT):
        out_ref[start : start + UNIT] = own_rows(
            start, dec_rows_ref, wide_ref[start // UNIT], cot_ref, acts_ref, mom_ref
        )


def momentum_kernel(
    dep, first_ref, wide_ref, dec_rows_ref, cot_ref, acts_ref, mom_ref, recv_ref, out_hbm, out_ref, sems
):
    copies = []
    for step in range(HALF // MOM_STEP):
        for start in range(step * MOM_STEP, (step + 1) * MOM_STEP, UNIT):
            rows = slice(start, start + UNIT)
            if start < FIRST:
                own = first_ref[rows]
            else:
                own = own_rows(start, dec_rows_ref, wide_ref[start // UNIT], cot_ref, acts_ref, mom_ref)
            out_ref[rows] = own + recv_ref[rows]
        rows = pl.ds(step * MOM_STEP, MOM_STEP)
        copy = pltpu.make_async_copy(out_ref.at[rows], out_hbm.at[0, rows], sems.at[step])
        copy.start()
        copies.append(copy)
    for copy in copies:
        copy.wait()


def update_kernel(
    dec_cols_ref, dec_rows_ref, coeffs_ref, weight_ref, update_hbm, new_hbm, wide_ref, update_ref, new_ref, sems
):
    decode_cols(coeffs_ref[...], dec_cols_ref, wide_ref, PAIRS[:3])
    copies = []
    for k in range(HALF // UNIT):
        rows = pl.ds(k * UNIT, UNIT)
        update = dot(dec_rows_ref[...], wide_ref[k])
        update_ref[rows] = update
        new_ref[rows] = (weight_ref[rows].astype(F32) - RATE * update).astype(BF)
        for i, (a, b) in enumerate(((update_ref, update_hbm), (new_ref, new_hbm))):
            copy = pltpu.make_async_copy(a.at[rows], b.at[rows], sems.at[2 * k + i])
            copy.start()
            copies.append(copy)
    for copy in copies:
        copy.wait()


def held(shape, dtype=F32):
    return pltpu.VMEM(shape, dtype)


def in_hbm(array):
    return pltpu.with_memory_space_constraint(array, pltpu.HBM)


def in_vmem(array):
    return pltpu.with_memory_space_constraint(array, pltpu.VMEM)


ANY = pl.BlockSpec(memory_space=pl.ANY)
INSIDE = pl.BlockSpec(memory_space=pltpu.VMEM)


def single(kernel, operands, specs, out_specs, out_shape, scratch, flops, nbytes):
    return pl.pallas_call(
        kernel,
        in_specs=specs,
        out_specs=out_specs,
        out_shape=out_shape,
        scratch_shapes=scratch,
        compiler_params=pltpu.CompilerParams(vmem_limit_bytes=VMEM_LIMIT),
        cost_estimate=pl.CostEstimate(flops=flops, bytes_accessed=nbytes, transcendentals=0),
    )(*operands)


COEFFS = jax.ShapeDtypeStruct((BANDS, ROWS_KEPT), F32)


def shift(axes, by):
    pairs = []
    for z in range(4):
        for y in range(4):
            for x in range(4):
                for core in range(2):
                    to = [z, y, x]
                    to[axes[core]] = (to[axes[core]] + by) % 4
                    pairs.append(((z * 16 + y * 4 + x) * 2 + core, (to[0] * 16 + to[1] * 4 + to[2]) * 2 + core))
    return pairs


def from_axis(x, axes):
    return [lax.ppermute(x, ("rep", "fsdp"), shift(axes, by)) for by in (1, 3, 2)]


def add_up(x, parts, beside):
    (a, b, c), _ = lax.optimization_barrier((parts, beside))
    return (x + c) + (a + b)


ORDERS = ((2, 1), (1, 0), (0, 2))
SWAP = ((0, 1), (1, 0))


def shards(acts, cotangent, weight, momentum):
    core = lax.axis_index("fsdp").astype(jnp.int32)
    enc_kv, enc_kv_cols = encoder_rows(KV), encoder_cols(KV)
    enc_rows, enc_cols = encoder_rows(UNIT), encoder_cols(UNIT)
    rows = (HALF, KV)
    SCALAR = pl.BlockSpec(memory_space=pltpu.SMEM)
    dma = lambda n: pltpu.SemaphoreType.DMA((n,))

    theirs, cot, z, acts_theirs = single(
        theirs_kernel,
        [(1 - core).reshape(1), *map(in_hbm, (cotangent, enc_kv, enc_cols, acts))],
        [SCALAR] + [ANY] * 4, [INSIDE] * 4,
        [COEFFS, held((TOK, KV), BF), held((2 * BANDS, TOK), BF), held((TOK, HALF), BF)],
        [held(enc_kv.shape, BF), held(enc_cols.shape, BF), dma(3 + len(THEIRS_CHUNKS))],
        2 * TOK * HALF * 192, 6_500_000,
    )
    got = lax.ppermute(theirs, "fsdp", SWAP)
    mine, acts_mine, mom = single(
        mine_kernel,
        [core.reshape(1), in_vmem(z), enc_rows, enc_kv_cols, enc_cols, *map(in_hbm, (acts, momentum))],
        [SCALAR] + [INSIDE] * 4 + [ANY] * 2, [INSIDE] * 3,
        [COEFFS, held((TOK, HALF), BF), held(rows)], [dma(len(MINE_ORDER))],
        2 * TOK * HALF * 300, 11_000_000,
    )
    coeffs = mine + got

    parts = from_axis(coeffs, ORDERS[0])
    partial = single(
        gradient_kernel, [coeffs, in_vmem(cot), in_vmem(acts_theirs)], [ANY, INSIDE, INSIDE],
        INSIDE, held(rows), [], 2 * TOK * HALF * KV, 12_000_000,
    )
    total, partial = lax.optimization_barrier((add_up(coeffs, parts, partial), partial))
    received = lax.ppermute(partial, "fsdp", SWAP)
    own = [in_vmem(x) for x in (cot, acts_mine, mom)]
    dec_rows = decoder_rows(PAIRS)
    first, wide = single(
        first_rows_kernel, [total, decoder_cols(PAIRS), dec_rows, coeffs, *own],
        [ANY] + [INSIDE] * 6, [INSIDE] * 2, [held((FIRST, KV)), held((HALF // UNIT, 6 * KEPT, KV), BF)],
        [], 2 * TOK * FIRST * 700, 12_000_000,
    )
    total = add_up(total, from_axis(total, ORDERS[1]), first)
    new_momentum = single(
        momentum_kernel, [total, *map(in_vmem, (first, wide)), dec_rows, *own, in_vmem(received)],
        [ANY] + [INSIDE] * 7, ANY, jax.ShapeDtypeStruct((1, HALF, KV), F32),
        [held(rows), dma(HALF // MOM_STEP)], 2 * TOK * (HALF - FIRST) * 700, 12_000_000,
    )
    total = add_up(total, from_axis(total, ORDERS[2]), new_momentum)

    update, new_weight = single(
        update_kernel, [decoder_cols(PAIRS[:3]), decoder_rows(PAIRS[:3]), total, weight],
        [INSIDE] * 4, [ANY] * 2, [jax.ShapeDtypeStruct(rows, F32), jax.ShapeDtypeStruct(rows, BF)],
        [held((HALF // UNIT, 3 * KEPT, KV), BF), held(rows), held(rows, BF), dma(2 * HALF // UNIT)],
        2 * HALF * KV * 400, 11_000_000,
    )
    return new_momentum, update, new_weight


def solution(mesh):
    in_specs = (
        P(("rep", "fsdp"), None),
        P(("rep", "fsdp"), None),
        P("fsdp", None),
        P("rep", "fsdp", None),
    )
    out_specs = (P("rep", "fsdp", None), P("fsdp", None), P("fsdp", None))
    return jax.shard_map(shards, mesh=mesh, in_specs=in_specs, out_specs=out_specs, check_vma=False)
```

```python
import jax
import jax.numpy as jnp
import ml_dtypes
import numpy as np
from jax import lax
from jax.experimental import pallas as pl
from jax.experimental.pallas import tpu as pltpu
from jax.sharding import PartitionSpec as P

SPAN = 64
KEEP = 8
BETA = 0.9
RATE = 0.02

TOK = 1024
KV = 512
HALF = 2560
UNIT = 256
KEPT = UNIT // SPAN * KEEP
BANDS = KV // SPAN * KEEP
ROWS_KEPT = HALF // SPAN * KEEP

THEIRS_CHUNKS = ((0, 512), (512, 1024), (1024, 1536), (1536, 2048), (2048, 2560))
MINE_CHUNKS = ((0, 1024), (1024, 2048), (2048, 2560))
MINE_ORDER = (("m", 0), ("a", 0), ("m", 1), ("m", 2), ("a", 1), ("m", 3), ("m", 4), ("a", 2))
MOM_STEP = 512
EARLY = 1024
FIRST = 1536
VMEM_LIMIT = 24 * 1024 * 1024

BF = jnp.bfloat16
F32 = jnp.float32


def dct_rows():
    freq = np.arange(KEEP)[:, None].astype(np.float64)
    cell = np.arange(SPAN)[None, :].astype(np.float64)
    scale = np.where(freq == 0, np.sqrt(1.0 / SPAN), np.sqrt(2.0 / SPAN))
    return (scale * np.cos(np.pi * (2.0 * cell + 1.0) * freq / (2.0 * SPAN))).astype(np.float32)


def basis_terms(size):
    out, rest = [], np.kron(np.eye(size // SPAN, dtype=np.float32), dct_rows())
    for _ in range(3):
        part = rest.astype(ml_dtypes.bfloat16)
        out.append(part)
        rest = rest - part.astype(np.float32)
    return out


PAIRS = ((0, 0), (0, 1), (1, 0), (1, 1), (0, 2), (2, 0))


def encoder_rows(size):
    return jnp.asarray(np.concatenate(basis_terms(size), axis=0))


def encoder_cols(size):
    return jnp.asarray(np.concatenate([t.T for t in basis_terms(size)], axis=1))


def decoder_cols(pairs):
    t = basis_terms(KV)
    return jnp.asarray(np.concatenate([t[j] for _, j in pairs], axis=0))


def decoder_rows(pairs):
    t = basis_terms(UNIT)
    return jnp.asarray(np.concatenate([t[i].T for i, _ in pairs], axis=1))


def pack(coeffs, out_ref):
    out_ref[:64] = coeffs[:, :128]
    out_ref[64:128] = coeffs[:, 128:256]
    out_ref[128:] = jnp.concatenate([coeffs[:32, 256:], coeffs[32:, 256:]], axis=1)


def unpack(packed):
    rest = jnp.concatenate([packed[128:, :64], packed[128:, 64:]], axis=0)
    return jnp.concatenate([packed[:64], packed[64:128], rest], axis=1)


def split(x):
    hi = x.astype(BF)
    rest = x - hi.astype(F32)
    mid = rest.astype(BF)
    lo = (rest - mid.astype(F32)).astype(BF)
    return hi, mid, lo


def dot(a, b, dims=((1,), (0,))):
    return lax.dot_general(a, b, (dims, ((), ())), preferred_element_type=F32)


def cross(product, rows, cols):
    total = None
    for i, j in reversed(PAIRS):
        piece = product[i * rows : (i + 1) * rows, j * cols : (j + 1) * cols]
        total = piece if total is None else total + piece
    return total


class Arrivals:
    def __init__(self, pairs, sems, ahead):
        self.copies = [pltpu.make_async_copy(a, b, sems.at[k]) for k, (a, b) in enumerate(pairs)]
        self.started, self.waited, self.ahead = 0, 0, ahead
        self.fill()

    def fill(self):
        while self.started < min(len(self.copies), self.waited + self.ahead):
            self.copies[self.started].start()
            self.started += 1

    def next(self):
        self.copies[self.waited].wait()
        self.waited += 1
        self.fill()


def encode_chunk(g, enc_cols):
    t = split(g)
    pieces = []
    for k in range(g.shape[1] // UNIT):
        stacked = jnp.concatenate([x[:, k * UNIT : (k + 1) * UNIT] for x in t], axis=0)
        pieces.append(cross(dot(stacked, enc_cols), BANDS, KEPT))
    return pieces


def momentum_rows(early_ref, late_ref, start):
    if start < EARLY:
        return early_ref[start : start + UNIT]
    return late_ref[start - EARLY : start - EARLY + UNIT]


def acts_copies(acts_hbm, acts_ref, half, chunks):
    pairs = []
    for lo, hi in chunks:
        start = pl.multiple_of(half * HALF + lo, UNIT)
        pairs.append((acts_hbm.at[:, pl.ds(start, hi - lo)], acts_ref.at[:, lo:hi]))
    return pairs


def encode_acts(z_ref, acts_ref, lo, hi):
    g = dot(z_ref[...], acts_ref[:, lo:hi])
    return g[BANDS:] + g[:BANDS]


def theirs_kernel(
    half, cot_hbm, enc_kv_hbm, enc_cols_hbm, acts_hbm, mom_hbm,
    theirs_ref, cot_ref, z_ref, acts_ref, mom_ref, enc_kv_ref, enc_cols_ref, sems,
):
    pairs = [(enc_kv_hbm, enc_kv_ref), (cot_hbm, cot_ref), (enc_cols_hbm, enc_cols_ref)]
    pairs += acts_copies(acts_hbm, acts_ref, half[0], THEIRS_CHUNKS)
    pairs.append((mom_hbm.at[0, :EARLY], mom_ref))
    arrivals = Arrivals(pairs, sems, 5)
    arrivals.next()
    arrivals.next()

    z = dot(enc_kv_ref[...], cot_ref[...], ((1,), (1,)))
    z_ref[...] = jnp.concatenate(split(z[2 * BANDS :] + z[BANDS : 2 * BANDS] + z[:BANDS])[:2], axis=0)
    arrivals.next()

    found, before = [], None
    for lo, hi in THEIRS_CHUNKS:
        arrivals.next()
        g = encode_acts(z_ref, acts_ref, lo, hi)
        if before is not None:
            found += encode_chunk(before, enc_cols_ref[...])
        before = g
    found += encode_chunk(before, enc_cols_ref[...])
    pack(jnp.concatenate(found, axis=1), theirs_ref)
    arrivals.next()


def mine_kernel(
    half, z_ref, early_ref, enc_rows_ref, enc_kv_cols_ref, enc_cols_ref, acts_hbm, mom_hbm,
    mine_ref, acts_ref, late_ref, sems,
):
    from_acts = acts_copies(acts_hbm, acts_ref, half[0], MINE_CHUNKS)
    from_mom = [
        (mom_hbm.at[0, pl.ds(start, MOM_STEP)], late_ref.at[pl.ds(start - EARLY, MOM_STEP)])
        for start in range(EARLY, HALF, MOM_STEP)
    ]
    copies = {("a", k): pair for k, pair in enumerate(from_acts)}
    copies |= {("m", EARLY // MOM_STEP + k): pair for k, pair in enumerate(from_mom)}
    arrivals = Arrivals([copies[c] for c in MINE_ORDER if c in copies], sems, 3)
    enc = enc_rows_ref[...]

    def encode_rows(start):
        m = momentum_rows(early_ref, late_ref, start)
        hi = m.astype(BF)
        a = dot(enc, hi)
        b = dot(enc[: 2 * KEPT], (m - hi.astype(F32)).astype(BF))
        return (b[KEPT:] + a[2 * KEPT :]) + (b[:KEPT] + a[KEPT : 2 * KEPT]) + a[:KEPT]

    def encode_cols(parts):
        n = len(parts) * KEPT
        terms = split(jnp.concatenate(parts, axis=0))
        return cross(dot(jnp.concatenate(terms, axis=0), enc_kv_cols_ref[...]), n, BANDS)

    found, from_rows, before = [], [], None
    for kind, k in MINE_ORDER + ((None, 0),):
        done = before
        if kind is not None:
            if (kind, k) in copies:
                arrivals.next()
            if kind == "a":
                before = kind, encode_acts(z_ref, acts_ref, *MINE_CHUNKS[k])
            else:
                before = kind, [encode_rows(k * MOM_STEP + i * UNIT) for i in range(MOM_STEP // UNIT)]
        if done is not None:
            if done[0] == "a":
                found += encode_chunk(done[1], enc_cols_ref[...])
            else:
                from_rows.append(encode_cols(done[1]))
    pack(jnp.concatenate(found, axis=1) + BETA * jnp.concatenate(from_rows, axis=0).T, mine_ref)


def own_kernel(dep, cot_ref, acts_ref, early_ref, late_ref, out_ref):
    for start in range(0, HALF, UNIT):
        rows = slice(start, start + UNIT)
        g = dot(acts_ref[:, rows], cot_ref[...], ((0,), (0,)))
        out_ref[rows] = BETA * momentum_rows(early_ref, late_ref, start) + g


def decode_cols(coeffs, dec_cols_ref, out_ref, pairs):
    t = split(coeffs)
    wide = dot(jnp.concatenate([t[i] for i, _ in pairs], axis=0), dec_cols_ref[...], ((0,), (0,)))
    w = split(wide)
    for g in range(HALF // UNIT):
        out_ref[g] = jnp.concatenate([w[j][g * KEPT : (g + 1) * KEPT] for _, j in pairs], axis=0)


def write_rows(first, last, own_ref, wide_ref, dec_rows_ref, cot_ref, acts_ref, out_hbm, out_ref, sems):
    copies = []
    for k, start in enumerate(range(first, last, UNIT)):
        rows, here = pl.ds(start, UNIT), pl.ds(start - first, UNIT)
        g = dot(acts_ref[:, rows], cot_ref[...], ((0,), (0,)))
        out_ref[here] = own_ref[rows] + g - dot(dec_rows_ref[...], wide_ref[start // UNIT])
        copy = pltpu.make_async_copy(out_ref.at[here], out_hbm.at[0, rows], sems.at[k])
        copy.start()
        copies.append(copy)
    for copy in copies:
        copy.wait()


def first_rows_kernel(
    dep, dec_cols_ref, dec_rows_ref, coeffs_ref, own_ref, cot_ref, acts_ref, out_hbm, wide_ref, out_ref, sems
):
    decode_cols(unpack(coeffs_ref[...]), dec_cols_ref, wide_ref, PAIRS)
    write_rows(0, FIRST, own_ref, wide_ref, dec_rows_ref, cot_ref, acts_ref, out_hbm, out_ref, sems)


def last_rows_kernel(
    dep, before, wide_ref, dec_rows_ref, own_ref, cot_ref, acts_ref, out_hbm, out_ref, sems
):
    write_rows(FIRST, HALF, own_ref, wide_ref, dec_rows_ref, cot_ref, acts_ref, out_hbm, out_ref, sems)


def update_kernel(
    dec_cols_ref, dec_rows_ref, coeffs_ref, weight_ref, update_hbm, new_hbm, wide_ref, update_ref, new_ref, sems
):
    decode_cols(unpack(coeffs_ref[...]), dec_cols_ref, wide_ref, PAIRS[:3])
    copies = []
    for k in range(HALF // UNIT):
        rows = pl.ds(k * UNIT, UNIT)
        update = dot(dec_rows_ref[...], wide_ref[k])
        update_ref[rows] = update
        new_ref[rows] = (weight_ref[rows].astype(F32) - RATE * update).astype(BF)
        for i, (a, b) in enumerate(((update_ref, update_hbm), (new_ref, new_hbm))):
            copy = pltpu.make_async_copy(a.at[rows], b.at[rows], sems.at[2 * k + i])
            copy.start()
            copies.append(copy)
    for copy in copies:
        copy.wait()


def held(shape, dtype=F32):
    return pltpu.VMEM(shape, dtype)


def in_hbm(array):
    return pltpu.with_memory_space_constraint(array, pltpu.HBM)


def in_vmem(array):
    return pltpu.with_memory_space_constraint(array, pltpu.VMEM)


ANY = pl.BlockSpec(memory_space=pl.ANY)
INSIDE = pl.BlockSpec(memory_space=pltpu.VMEM)


def single(kernel, operands, specs, out_specs, out_shape, scratch, flops, nbytes, aliases={}):
    return pl.pallas_call(
        kernel,
        in_specs=specs,
        out_specs=out_specs,
        out_shape=out_shape,
        scratch_shapes=scratch,
        input_output_aliases=aliases,
        compiler_params=pltpu.CompilerParams(vmem_limit_bytes=VMEM_LIMIT),
        cost_estimate=pl.CostEstimate(flops=flops, bytes_accessed=nbytes, transcendentals=0),
    )(*operands)


COEFFS = jax.ShapeDtypeStruct((BANDS * ROWS_KEPT // 128, 128), F32)


def shift(axes, by):
    pairs = []
    for z in range(4):
        for y in range(4):
            for x in range(4):
                for core in range(2):
                    to = [z, y, x]
                    to[axes[core]] = (to[axes[core]] + by) % 4
                    pairs.append(((z * 16 + y * 4 + x) * 2 + core, (to[0] * 16 + to[1] * 4 + to[2]) * 2 + core))
    return pairs


def from_axis(x, axes, order=(2, 3, 1)):
    return [lax.ppermute(x, ("rep", "fsdp"), shift(axes, by)) for by in order]


def add_up(x, parts, beside):
    (a, b, c), _ = lax.optimization_barrier((parts, beside))
    return (x + c) + (a + b)


ORDERS = ((2, 1), (1, 0), (0, 2))
SWAP = ((0, 1), (1, 0))


def shards(acts, cotangent, weight, momentum):
    core = lax.axis_index("fsdp").astype(jnp.int32)
    enc_kv, enc_kv_cols = encoder_rows(KV), encoder_cols(KV)
    enc_rows, enc_cols = encoder_rows(UNIT), encoder_cols(UNIT)
    rows = (HALF, KV)
    SCALAR = pl.BlockSpec(memory_space=pltpu.SMEM)
    dma = lambda n: pltpu.SemaphoreType.DMA((n,))

    theirs, cot, z, acts_theirs, early = single(
        theirs_kernel,
        [(1 - core).reshape(1), *map(in_hbm, (cotangent, enc_kv, enc_cols, acts, momentum))],
        [SCALAR] + [ANY] * 5, [INSIDE] * 5,
        [COEFFS, held((TOK, KV), BF), held((2 * BANDS, TOK), BF), held((TOK, HALF), BF), held((EARLY, KV))],
        [held(enc_kv.shape, BF), held(enc_cols.shape, BF), dma(4 + len(THEIRS_CHUNKS))],
        2 * TOK * HALF * 192, 6_500_000,
    )
    got = lax.ppermute(theirs, "fsdp", SWAP)
    mine, acts_mine, late = single(
        mine_kernel,
        [core.reshape(1), in_vmem(z), in_vmem(early), enc_rows, enc_kv_cols, enc_cols, *map(in_hbm, (acts, momentum))],
        [SCALAR] + [INSIDE] * 5 + [ANY] * 2, [INSIDE] * 3,
        [COEFFS, held((TOK, HALF), BF), held((HALF - EARLY, KV))], [dma(len(MINE_ORDER))],
        2 * TOK * HALF * 300, 11_000_000,
    )
    coeffs, acts_theirs, cot_theirs = lax.optimization_barrier((mine + got, acts_theirs, cot))
    acts_got, cot_got = (lax.ppermute(x, "fsdp", SWAP) for x in (acts_theirs, cot_theirs))

    parts = from_axis(coeffs, ORDERS[0])
    own = single(
        own_kernel, [coeffs, *map(in_vmem, (cot, acts_mine, early, late))], [ANY] + [INSIDE] * 4,
        INSIDE, held(rows), [], 2 * TOK * HALF * KV, 12_000_000,
    )
    total = add_up(coeffs, parts, own)
    dec_rows = decoder_rows(PAIRS)
    momentum_shape = jax.ShapeDtypeStruct((1, HALF, KV), F32)
    others = [in_vmem(x) for x in (own, cot_got, acts_got)]
    new_momentum, wide = single(
        first_rows_kernel, [total, decoder_cols(PAIRS), dec_rows, coeffs, *others],
        [ANY] + [INSIDE] * 6, [ANY, INSIDE], [momentum_shape, held((HALF // UNIT, 6 * KEPT, KV), BF)],
        [held((FIRST, KV)), dma(FIRST // UNIT)], 2 * TOK * FIRST * 700, 12_000_000,
    )
    total = add_up(total, from_axis(total, ORDERS[1]), new_momentum)
    new_momentum = single(
        last_rows_kernel, [total, new_momentum, in_vmem(wide), dec_rows, *others],
        [ANY] * 2 + [INSIDE] * 5, ANY, momentum_shape,
        [held((HALF - FIRST, KV)), dma((HALF - FIRST) // UNIT)], 2 * TOK * (HALF - FIRST) * 700, 8_000_000,
        {1: 0},
    )
    total = add_up(total, from_axis(total, ORDERS[2], (3, 1, 2)), new_momentum)

    update, new_weight = single(
        update_kernel, [decoder_cols(PAIRS[:3]), decoder_rows(PAIRS[:3]), total, weight],
        [INSIDE] * 4, [ANY] * 2, [jax.ShapeDtypeStruct(rows, F32), jax.ShapeDtypeStruct(rows, BF)],
        [held((HALF // UNIT, 3 * KEPT, KV), BF), held(rows), held(rows, BF), dma(2 * HALF // UNIT)],
        2 * HALF * KV * 400, 11_000_000,
    )
    return new_momentum, update, new_weight


def solution(mesh):
    in_specs = (
        P(("rep", "fsdp"), None),
        P(("rep", "fsdp"), None),
        P("fsdp", None),
        P("rep", "fsdp", None),
    )
    out_specs = (P("rep", "fsdp", None), P("fsdp", None), P("fsdp", None))
    return jax.shard_map(shards, mesh=mesh, in_specs=in_specs, out_specs=out_specs, check_vma=False)
```

```python
import jax
import jax.numpy as jnp
import ml_dtypes
import numpy as np
from jax import lax
from jax.experimental import pallas as pl
from jax.experimental.pallas import tpu as pltpu
from jax.sharding import PartitionSpec as P

SPAN = 64
KEEP = 8
BETA = 0.9
RATE = 0.02

TOK = 1024
KV = 512
HALF = 2560
UNIT = 256
KEPT = UNIT // SPAN * KEEP
BANDS = KV // SPAN * KEEP
ROWS_KEPT = HALF // SPAN * KEEP

THEIRS_CHUNKS = ((0, 512), (512, 1024), (1024, 1536), (1536, 2048), (2048, 2560))
MINE_CHUNKS = ((0, 1024), (1024, 2048), (2048, 2560))
MINE_ORDER = (("m", 0), ("a", 0), ("m", 1), ("m", 2), ("a", 1), ("m", 3), ("m", 4), ("a", 2))
MOM_STEP = 512
EARLY = 1024
FIRST = 1536
VMEM_LIMIT = 24 * 1024 * 1024

BF = jnp.bfloat16
F32 = jnp.float32


def dct_rows():
    freq = np.arange(KEEP)[:, None].astype(np.float64)
    cell = np.arange(SPAN)[None, :].astype(np.float64)
    scale = np.where(freq == 0, np.sqrt(1.0 / SPAN), np.sqrt(2.0 / SPAN))
    return (scale * np.cos(np.pi * (2.0 * cell + 1.0) * freq / (2.0 * SPAN))).astype(np.float32)


def basis_terms(size):
    out, rest = [], np.kron(np.eye(size // SPAN, dtype=np.float32), dct_rows())
    for _ in range(3):
        part = rest.astype(ml_dtypes.bfloat16)
        out.append(part)
        rest = rest - part.astype(np.float32)
    return out


PAIRS = ((0, 0), (0, 1), (1, 0), (1, 1), (0, 2), (2, 0))


def encoder_rows(size):
    return jnp.asarray(np.concatenate(basis_terms(size), axis=0))


def encoder_cols(size):
    return jnp.asarray(np.concatenate([t.T for t in basis_terms(size)], axis=1))


def decoder_cols(pairs):
    t = basis_terms(KV)
    return jnp.asarray(np.concatenate([t[j] for _, j in pairs], axis=0))


def decoder_rows(pairs):
    t = basis_terms(UNIT)
    return jnp.asarray(np.concatenate([t[i].T for i, _ in pairs], axis=1))


def pack(coeffs, out_ref):
    out_ref[:64] = coeffs[:, :128]
    out_ref[64:128] = coeffs[:, 128:256]
    out_ref[128:] = jnp.concatenate([coeffs[:32, 256:], coeffs[32:, 256:]], axis=1)


def unpack(packed):
    rest = jnp.concatenate([packed[128:, :64], packed[128:, 64:]], axis=0)
    return jnp.concatenate([packed[:64], packed[64:128], rest], axis=1)


def split(x):
    hi = x.astype(BF)
    rest = x - hi.astype(F32)
    mid = rest.astype(BF)
    lo = (rest - mid.astype(F32)).astype(BF)
    return hi, mid, lo


def dot(a, b, dims=((1,), (0,))):
    return lax.dot_general(a, b, (dims, ((), ())), preferred_element_type=F32)


def cross(product, rows, cols):
    total = None
    for i, j in reversed(PAIRS):
        piece = product[i * rows : (i + 1) * rows, j * cols : (j + 1) * cols]
        total = piece if total is None else total + piece
    return total


class Arrivals:
    def __init__(self, pairs, sems, ahead):
        self.copies = [pltpu.make_async_copy(a, b, sems.at[k]) for k, (a, b) in enumerate(pairs)]
        self.started, self.waited, self.ahead = 0, 0, ahead
        self.fill()

    def fill(self):
        while self.started < min(len(self.copies), self.waited + self.ahead):
            self.copies[self.started].start()
            self.started += 1

    def next(self):
        self.copies[self.waited].wait()
        self.waited += 1
        self.fill()


def encode_chunk(g, enc_cols):
    t = split(g)
    pieces = []
    for k in range(g.shape[1] // UNIT):
        stacked = jnp.concatenate([x[:, k * UNIT : (k + 1) * UNIT] for x in t], axis=0)
        pieces.append(cross(dot(stacked, enc_cols), BANDS, KEPT))
    return pieces


def momentum_rows(early_ref, late_ref, start):
    if start < EARLY:
        return early_ref[start : start + UNIT]
    return late_ref[start - EARLY : start - EARLY + UNIT]


def acts_copies(acts_hbm, acts_ref, half, chunks):
    pairs = []
    for lo, hi in chunks:
        start = pl.multiple_of(half * HALF + lo, UNIT)
        pairs.append((acts_hbm.at[:, pl.ds(start, hi - lo)], acts_ref.at[:, lo:hi]))
    return pairs


def encode_acts(z_ref, acts_ref, lo, hi):
    g = dot(z_ref[...], acts_ref[:, lo:hi])
    return g[BANDS:] + g[:BANDS]


def theirs_kernel(
    half, cot_hbm, enc_kv_hbm, enc_cols_hbm, acts_hbm, mom_hbm,
    theirs_ref, cot_ref, z_ref, acts_ref, mom_ref, enc_kv_ref, enc_cols_ref, sems,
):
    pairs = [(enc_kv_hbm, enc_kv_ref), (cot_hbm, cot_ref), (enc_cols_hbm, enc_cols_ref)]
    pairs += acts_copies(acts_hbm, acts_ref, half[0], THEIRS_CHUNKS)
    pairs.append((mom_hbm.at[0, :EARLY], mom_ref))
    arrivals = Arrivals(pairs, sems, 5)
    arrivals.next()
    arrivals.next()

    z = dot(enc_kv_ref[...], cot_ref[...], ((1,), (1,)))
    z_ref[...] = jnp.concatenate(split(z[2 * BANDS :] + z[BANDS : 2 * BANDS] + z[:BANDS])[:2], axis=0)
    arrivals.next()

    found, before = [], None
    for lo, hi in THEIRS_CHUNKS:
        arrivals.next()
        g = encode_acts(z_ref, acts_ref, lo, hi)
        if before is not None:
            found += encode_chunk(before, enc_cols_ref[...])
        before = g
    found += encode_chunk(before, enc_cols_ref[...])
    pack(jnp.concatenate(found, axis=1), theirs_ref)
    arrivals.next()


def mine_kernel(
    half, z_ref, early_ref, enc_rows_ref, enc_kv_cols_ref, enc_cols_ref, acts_hbm, mom_hbm,
    mine_ref, acts_ref, late_ref, sems,
):
    from_acts = acts_copies(acts_hbm, acts_ref, half[0], MINE_CHUNKS)
    from_mom = [
        (mom_hbm.at[0, pl.ds(start, MOM_STEP)], late_ref.at[pl.ds(start - EARLY, MOM_STEP)])
        for start in range(EARLY, HALF, MOM_STEP)
    ]
    copies = {("a", k): pair for k, pair in enumerate(from_acts)}
    copies |= {("m", EARLY // MOM_STEP + k): pair for k, pair in enumerate(from_mom)}
    arrivals = Arrivals([copies[c] for c in MINE_ORDER if c in copies], sems, 3)
    enc = enc_rows_ref[...]

    def encode_rows(start):
        m = momentum_rows(early_ref, late_ref, start)
        hi = m.astype(BF)
        a = dot(enc, hi)
        b = dot(enc[: 2 * KEPT], (m - hi.astype(F32)).astype(BF))
        return (b[KEPT:] + a[2 * KEPT :]) + (b[:KEPT] + a[KEPT : 2 * KEPT]) + a[:KEPT]

    def encode_cols(parts):
        n = len(parts) * KEPT
        terms = split(jnp.concatenate(parts, axis=0))
        return cross(dot(jnp.concatenate(terms, axis=0), enc_kv_cols_ref[...]), n, BANDS)

    found, from_rows, before = [], [], None
    for kind, k in MINE_ORDER + ((None, 0),):
        done = before
        if kind is not None:
            if (kind, k) in copies:
                arrivals.next()
            if kind == "a":
                before = kind, encode_acts(z_ref, acts_ref, *MINE_CHUNKS[k])
            else:
                before = kind, [encode_rows(k * MOM_STEP + i * UNIT) for i in range(MOM_STEP // UNIT)]
        if done is not None:
            if done[0] == "a":
                found += encode_chunk(done[1], enc_cols_ref[...])
            else:
                from_rows.append(encode_cols(done[1]))
    pack(jnp.concatenate(found, axis=1) + BETA * jnp.concatenate(from_rows, axis=0).T, mine_ref)


def own_kernel(dep, cot_ref, acts_ref, early_ref, late_ref, out_ref):
    for start in range(0, HALF, UNIT):
        rows = slice(start, start + UNIT)
        g = dot(acts_ref[:, rows], cot_ref[...], ((0,), (0,)))
        out_ref[rows] = BETA * momentum_rows(early_ref, late_ref, start) + g


def decode_cols(coeffs, dec_cols_ref, out_ref, pairs):
    t = split(coeffs)
    wide = dot(jnp.concatenate([t[i] for i, _ in pairs], axis=0), dec_cols_ref[...], ((0,), (0,)))
    w = split(wide)
    for g in range(HALF // UNIT):
        out_ref[g] = jnp.concatenate([w[j][g * KEPT : (g + 1) * KEPT] for _, j in pairs], axis=0)


def write_rows(first, last, own_ref, wide_ref, dec_rows_ref, cot_ref, acts_ref, out_hbm, out_ref, sems):
    copies = []
    for k, start in enumerate(range(first, last, UNIT)):
        rows, here = pl.ds(start, UNIT), pl.ds(start - first, UNIT)
        g = dot(acts_ref[:, rows], cot_ref[...], ((0,), (0,)))
        out_ref[here] = own_ref[rows] + g - dot(dec_rows_ref[...], wide_ref[start // UNIT])
        copy = pltpu.make_async_copy(out_ref.at[here], out_hbm.at[0, rows], sems.at[k])
        copy.start()
        copies.append(copy)
    for copy in copies:
        copy.wait()


def first_rows_kernel(
    dep, dec_cols_ref, dec_rows_ref, coeffs_ref, own_ref, cot_ref, acts_ref, out_hbm, wide_ref, out_ref, sems
):
    decode_cols(unpack(coeffs_ref[...]), dec_cols_ref, wide_ref, PAIRS)
    write_rows(0, FIRST, own_ref, wide_ref, dec_rows_ref, cot_ref, acts_ref, out_hbm, out_ref, sems)


def last_rows_kernel(
    dep, before, wide_ref, dec_rows_ref, own_ref, cot_ref, acts_ref, out_hbm, out_ref, sems
):
    write_rows(FIRST, HALF, own_ref, wide_ref, dec_rows_ref, cot_ref, acts_ref, out_hbm, out_ref, sems)


def update_kernel(
    dec_cols_ref, dec_rows_ref, coeffs_ref, weight_ref, update_hbm, new_hbm, wide_ref, update_ref, new_ref, sems
):
    decode_cols(unpack(coeffs_ref[...]), dec_cols_ref, wide_ref, PAIRS[:3])
    copies = []
    for k in range(HALF // UNIT):
        rows = pl.ds(k * UNIT, UNIT)
        update = dot(dec_rows_ref[...], wide_ref[k])
        update_ref[rows] = update
        new_ref[rows] = (weight_ref[rows].astype(F32) - RATE * update).astype(BF)
        for i, (a, b) in enumerate(((update_ref, update_hbm), (new_ref, new_hbm))):
            copy = pltpu.make_async_copy(a.at[rows], b.at[rows], sems.at[2 * k + i])
            copy.start()
            copies.append(copy)
    for copy in copies:
        copy.wait()


def held(shape, dtype=F32):
    return pltpu.VMEM(shape, dtype)


def in_hbm(array):
    return pltpu.with_memory_space_constraint(array, pltpu.HBM)


def in_vmem(array):
    return pltpu.with_memory_space_constraint(array, pltpu.VMEM)


ANY = pl.BlockSpec(memory_space=pl.ANY)
INSIDE = pl.BlockSpec(memory_space=pltpu.VMEM)


def single(kernel, operands, specs, out_specs, out_shape, scratch, flops, nbytes, aliases={}):
    return pl.pallas_call(
        kernel,
        in_specs=specs,
        out_specs=out_specs,
        out_shape=out_shape,
        scratch_shapes=scratch,
        input_output_aliases=aliases,
        compiler_params=pltpu.CompilerParams(vmem_limit_bytes=VMEM_LIMIT),
        cost_estimate=pl.CostEstimate(flops=flops, bytes_accessed=nbytes, transcendentals=0),
    )(*operands)


COEFFS = jax.ShapeDtypeStruct((BANDS * ROWS_KEPT // 128, 128), F32)


def shift(axes, by):
    pairs = []
    for z in range(4):
        for y in range(4):
            for x in range(4):
                for core in range(2):
                    to = [z, y, x]
                    to[axes[core]] = (to[axes[core]] + by) % 4
                    pairs.append(((z * 16 + y * 4 + x) * 2 + core, (to[0] * 16 + to[1] * 4 + to[2]) * 2 + core))
    return pairs


def from_axis(x, axes, order=(3, 2, 1)):
    return [lax.ppermute(x, ("rep", "fsdp"), shift(axes, by)) for by in order]


def add_up(x, parts, beside):
    (a, b, c), _ = lax.optimization_barrier((parts, beside))
    return (x + c) + (a + b)


ORDERS = ((2, 1), (1, 0), (0, 2))
SWAP = ((0, 1), (1, 0))


def shards(acts, cotangent, weight, momentum):
    core = lax.axis_index("fsdp").astype(jnp.int32)
    enc_kv, enc_kv_cols = encoder_rows(KV), encoder_cols(KV)
    enc_rows, enc_cols = encoder_rows(UNIT), encoder_cols(UNIT)
    rows = (HALF, KV)
    SCALAR = pl.BlockSpec(memory_space=pltpu.SMEM)
    dma = lambda n: pltpu.SemaphoreType.DMA((n,))

    theirs, cot, z, acts_theirs, early = single(
        theirs_kernel,
        [(1 - core).reshape(1), *map(in_hbm, (cotangent, enc_kv, enc_cols, acts, momentum))],
        [SCALAR] + [ANY] * 5, [INSIDE] * 5,
        [COEFFS, held((TOK, KV), BF), held((2 * BANDS, TOK), BF), held((TOK, HALF), BF), held((EARLY, KV))],
        [held(enc_kv.shape, BF), held(enc_cols.shape, BF), dma(4 + len(THEIRS_CHUNKS))],
        2 * TOK * HALF * 192, 6_500_000,
    )
    got = lax.ppermute(theirs, "fsdp", SWAP)
    mine, acts_mine, late = single(
        mine_kernel,
        [core.reshape(1), in_vmem(z), in_vmem(early), enc_rows, enc_kv_cols, enc_cols, *map(in_hbm, (acts, momentum))],
        [SCALAR] + [INSIDE] * 5 + [ANY] * 2, [INSIDE] * 3,
        [COEFFS, held((TOK, HALF), BF), held((HALF - EARLY, KV))], [dma(len(MINE_ORDER))],
        2 * TOK * HALF * 300, 11_000_000,
    )
    coeffs, acts_theirs, cot_theirs = lax.optimization_barrier((mine + got, acts_theirs, cot))
    acts_got, cot_got = (lax.ppermute(x, "fsdp", SWAP) for x in (acts_theirs, cot_theirs))

    parts = from_axis(coeffs, ORDERS[0])
    own = single(
        own_kernel, [coeffs, *map(in_vmem, (cot, acts_mine, early, late))], [ANY] + [INSIDE] * 4,
        INSIDE, held(rows), [], 2 * TOK * HALF * KV, 12_000_000,
    )
    total = add_up(coeffs, parts, own)
    dec_rows = decoder_rows(PAIRS)
    momentum_shape = jax.ShapeDtypeStruct((1, HALF, KV), F32)
    others = [in_vmem(x) for x in (own, cot_got, acts_got)]
    new_momentum, wide = single(
        first_rows_kernel, [total, decoder_cols(PAIRS), dec_rows, coeffs, *others],
        [ANY] + [INSIDE] * 6, [ANY, INSIDE], [momentum_shape, held((HALF // UNIT, 6 * KEPT, KV), BF)],
        [held((FIRST, KV)), dma(FIRST // UNIT)], 2 * TOK * FIRST * 700, 12_000_000,
    )
    total = add_up(total, from_axis(total, ORDERS[1]), new_momentum)
    new_momentum = single(
        last_rows_kernel, [total, new_momentum, in_vmem(wide), dec_rows, *others],
        [ANY] * 2 + [INSIDE] * 5, ANY, momentum_shape,
        [held((HALF - FIRST, KV)), dma((HALF - FIRST) // UNIT)], 2 * TOK * (HALF - FIRST) * 700, 8_000_000,
        {1: 0},
    )
    total = add_up(total, from_axis(total, ORDERS[2], (3, 1, 2)), new_momentum)

    update, new_weight = single(
        update_kernel, [decoder_cols(PAIRS[:3]), decoder_rows(PAIRS[:3]), total, weight],
        [INSIDE] * 4, [ANY] * 2, [jax.ShapeDtypeStruct(rows, F32), jax.ShapeDtypeStruct(rows, BF)],
        [held((HALF // UNIT, 3 * KEPT, KV), BF), held(rows), held(rows, BF), dma(2 * HALF // UNIT)],
        2 * HALF * KV * 400, 11_000_000,
    )
    return new_momentum, update, new_weight


def solution(mesh):
    in_specs = (
        P(("rep", "fsdp"), None),
        P(("rep", "fsdp"), None),
        P("fsdp", None),
        P("rep", "fsdp", None),
    )
    out_specs = (P("rep", "fsdp", None), P("fsdp", None), P("fsdp", None))
    return jax.shard_map(shards, mesh=mesh, in_specs=in_specs, out_specs=out_specs, check_vma=False)
```

```python
import jax
import jax.numpy as jnp
import ml_dtypes
import numpy as np
from jax import lax
from jax.experimental import pallas as pl
from jax.experimental.pallas import tpu as pltpu
from jax.sharding import PartitionSpec as P

SPAN = 64
KEEP = 8
BETA = 0.9
RATE = 0.02

TOK = 1024
KV = 512
HALF = 2560
UNIT = 256
KEPT = UNIT // SPAN * KEEP
BANDS = KV // SPAN * KEEP
ROWS_KEPT = HALF // SPAN * KEEP

THEIRS_CHUNKS = ((0, 512), (512, 1024), (1024, 1536), (1536, 2048), (2048, 2560))
MINE_CHUNKS = ((0, 1280), (1280, 2560))
MINE_ORDER = (("m", 0), ("m", 1), ("a", 0), ("m", 2), ("m", 3), ("a", 1), ("m", 4))
MOM_STEP = 512
EARLY = 1024
FIRST = 1536
VMEM_LIMIT = 24 * 1024 * 1024

BF = jnp.bfloat16
F32 = jnp.float32


def dct_rows():
    freq = np.arange(KEEP)[:, None].astype(np.float64)
    cell = np.arange(SPAN)[None, :].astype(np.float64)
    scale = np.where(freq == 0, np.sqrt(1.0 / SPAN), np.sqrt(2.0 / SPAN))
    return (scale * np.cos(np.pi * (2.0 * cell + 1.0) * freq / (2.0 * SPAN))).astype(np.float32)


def basis_terms(size):
    out, rest = [], np.kron(np.eye(size // SPAN, dtype=np.float32), dct_rows())
    for _ in range(3):
        part = rest.astype(ml_dtypes.bfloat16)
        out.append(part)
        rest = rest - part.astype(np.float32)
    return out


PAIRS = ((0, 0), (0, 1), (1, 0), (1, 1), (0, 2), (2, 0))


def encoder_rows(size):
    return jnp.asarray(np.concatenate(basis_terms(size), axis=0))


def encoder_cols(size):
    return jnp.asarray(np.concatenate([t.T for t in basis_terms(size)], axis=1))


def decoder_cols(pairs):
    t = basis_terms(KV)
    return jnp.asarray(np.concatenate([t[j] for _, j in pairs], axis=0))


def decoder_rows(pairs):
    t = basis_terms(UNIT)
    return jnp.asarray(np.concatenate([t[i].T for i, _ in pairs], axis=1))


def pack(coeffs, out_ref):
    out_ref[:64] = coeffs[:, :128]
    out_ref[64:128] = coeffs[:, 128:256]
    out_ref[128:] = jnp.concatenate([coeffs[:32, 256:], coeffs[32:, 256:]], axis=1)


def unpack(packed):
    rest = jnp.concatenate([packed[128:, :64], packed[128:, 64:]], axis=0)
    return jnp.concatenate([packed[:64], packed[64:128], rest], axis=1)


def split(x):
    hi = x.astype(BF)
    rest = x - hi.astype(F32)
    mid = rest.astype(BF)
    lo = (rest - mid.astype(F32)).astype(BF)
    return hi, mid, lo


def dot(a, b, dims=((1,), (0,))):
    return lax.dot_general(a, b, (dims, ((), ())), preferred_element_type=F32)


def cross(product, rows, cols):
    total = None
    for i, j in reversed(PAIRS):
        piece = product[i * rows : (i + 1) * rows, j * cols : (j + 1) * cols]
        total = piece if total is None else total + piece
    return total


class Arrivals:
    def __init__(self, pairs, sems, ahead):
        self.copies = [pltpu.make_async_copy(a, b, sems.at[k]) for k, (a, b) in enumerate(pairs)]
        self.started, self.waited, self.ahead = 0, 0, ahead
        self.fill()

    def fill(self):
        while self.started < min(len(self.copies), self.waited + self.ahead):
            self.copies[self.started].start()
            self.started += 1

    def next(self):
        self.copies[self.waited].wait()
        self.waited += 1
        self.fill()


def encode_chunk(g, enc_cols):
    t = split(g)
    pieces = []
    for k in range(g.shape[1] // UNIT):
        stacked = jnp.concatenate([x[:, k * UNIT : (k + 1) * UNIT] for x in t], axis=0)
        pieces.append(cross(dot(stacked, enc_cols), BANDS, KEPT))
    return pieces


def momentum_rows(early_ref, late_ref, start):
    if start < EARLY:
        return early_ref[start : start + UNIT]
    return late_ref[start - EARLY : start - EARLY + UNIT]


def acts_copies(acts_hbm, acts_ref, half, chunks):
    pairs = []
    for lo, hi in chunks:
        start = pl.multiple_of(half * HALF + lo, UNIT)
        pairs.append((acts_hbm.at[:, pl.ds(start, hi - lo)], acts_ref.at[:, lo:hi]))
    return pairs


def encode_acts(z_ref, acts_ref, lo, hi):
    g = dot(z_ref[...], acts_ref[:, lo:hi])
    return g[BANDS:] + g[:BANDS]


def theirs_kernel(
    half, cot_hbm, enc_kv_hbm, enc_cols_hbm, acts_hbm, mom_hbm,
    theirs_ref, cot_ref, z_ref, acts_ref, mom_ref, enc_kv_ref, enc_cols_ref, sems,
):
    pairs = [(enc_kv_hbm, enc_kv_ref), (cot_hbm, cot_ref), (enc_cols_hbm, enc_cols_ref)]
    pairs += acts_copies(acts_hbm, acts_ref, half[0], THEIRS_CHUNKS)
    pairs.append((mom_hbm.at[0, :EARLY], mom_ref))
    arrivals = Arrivals(pairs, sems, 5)
    arrivals.next()
    arrivals.next()

    z = dot(enc_kv_ref[...], cot_ref[...], ((1,), (1,)))
    z_ref[...] = jnp.concatenate(split(z[2 * BANDS :] + z[BANDS : 2 * BANDS] + z[:BANDS])[:2], axis=0)
    arrivals.next()

    found, before = [], None
    for lo, hi in THEIRS_CHUNKS:
        arrivals.next()
        g = encode_acts(z_ref, acts_ref, lo, hi)
        if before is not None:
            found += encode_chunk(before, enc_cols_ref[...])
        before = g
    found += encode_chunk(before, enc_cols_ref[...])
    pack(jnp.concatenate(found, axis=1), theirs_ref)
    arrivals.next()


def mine_kernel(
    half, z_ref, early_ref, enc_rows_ref, enc_kv_cols_ref, enc_cols_ref, acts_hbm, mom_hbm,
    mine_ref, acts_ref, late_ref, sems,
):
    from_acts = acts_copies(acts_hbm, acts_ref, half[0], MINE_CHUNKS)
    from_mom = [
        (mom_hbm.at[0, pl.ds(start, MOM_STEP)], late_ref.at[pl.ds(start - EARLY, MOM_STEP)])
        for start in range(EARLY, HALF, MOM_STEP)
    ]
    copies = {("a", k): pair for k, pair in enumerate(from_acts)}
    copies |= {("m", EARLY // MOM_STEP + k): pair for k, pair in enumerate(from_mom)}
    arrivals = Arrivals([copies[c] for c in MINE_ORDER if c in copies], sems, 3)
    enc = enc_rows_ref[...]

    def encode_rows(start):
        m = momentum_rows(early_ref, late_ref, start)
        hi = m.astype(BF)
        a = dot(enc, hi)
        b = dot(enc[: 2 * KEPT], (m - hi.astype(F32)).astype(BF))
        return (b[KEPT:] + a[2 * KEPT :]) + (b[:KEPT] + a[KEPT : 2 * KEPT]) + a[:KEPT]

    def encode_cols(parts):
        n = len(parts) * KEPT
        terms = split(jnp.concatenate(parts, axis=0))
        return cross(dot(jnp.concatenate(terms, axis=0), enc_kv_cols_ref[...]), n, BANDS)

    found, from_rows, before = [], [], None
    for kind, k in MINE_ORDER + ((None, 0),):
        done = before
        if kind is not None:
            if (kind, k) in copies:
                arrivals.next()
            if kind == "a":
                before = kind, encode_acts(z_ref, acts_ref, *MINE_CHUNKS[k])
            else:
                before = kind, [encode_rows(k * MOM_STEP + i * UNIT) for i in range(MOM_STEP // UNIT)]
        if done is not None:
            if done[0] == "a":
                found += encode_chunk(done[1], enc_cols_ref[...])
            else:
                from_rows.append(encode_cols(done[1]))
    pack(jnp.concatenate(found, axis=1) + BETA * jnp.concatenate(from_rows, axis=0).T, mine_ref)


def own_kernel(dep, cot_ref, acts_ref, early_ref, late_ref, out_ref):
    for start in range(0, HALF, UNIT):
        rows = slice(start, start + UNIT)
        g = dot(acts_ref[:, rows], cot_ref[...], ((0,), (0,)))
        out_ref[rows] = BETA * momentum_rows(early_ref, late_ref, start) + g


def decode_cols(coeffs, dec_cols_ref, out_ref, pairs):
    t = split(coeffs)
    wide = dot(jnp.concatenate([t[i] for i, _ in pairs], axis=0), dec_cols_ref[...], ((0,), (0,)))
    w = split(wide)
    for g in range(HALF // UNIT):
        out_ref[g] = jnp.concatenate([w[j][g * KEPT : (g + 1) * KEPT] for _, j in pairs], axis=0)


def write_rows(first, last, own_ref, wide_ref, dec_rows_ref, cot_ref, acts_ref, out_hbm, out_ref, sems):
    copies = []
    for k, start in enumerate(range(first, last, UNIT)):
        rows, here = pl.ds(start, UNIT), pl.ds(start - first, UNIT)
        g = dot(acts_ref[:, rows], cot_ref[...], ((0,), (0,)))
        out_ref[here] = own_ref[rows] + g - dot(dec_rows_ref[...], wide_ref[start // UNIT])
        copy = pltpu.make_async_copy(out_ref.at[here], out_hbm.at[0, rows], sems.at[k])
        copy.start()
        copies.append(copy)
    for copy in copies:
        copy.wait()


def first_rows_kernel(
    dep, dec_cols_ref, dec_rows_ref, coeffs_ref, own_ref, cot_ref, acts_ref, out_hbm, wide_ref, out_ref, sems
):
    decode_cols(unpack(coeffs_ref[...]), dec_cols_ref, wide_ref, PAIRS)
    write_rows(0, FIRST, own_ref, wide_ref, dec_rows_ref, cot_ref, acts_ref, out_hbm, out_ref, sems)


def last_rows_kernel(
    dep, before, wide_ref, dec_rows_ref, own_ref, cot_ref, acts_ref, out_hbm, out_ref, sems
):
    write_rows(FIRST, HALF, own_ref, wide_ref, dec_rows_ref, cot_ref, acts_ref, out_hbm, out_ref, sems)


def update_kernel(
    dec_cols_ref, dec_rows_ref, coeffs_ref, weight_ref, update_hbm, new_hbm, wide_ref, update_ref, new_ref, sems
):
    decode_cols(unpack(coeffs_ref[...]), dec_cols_ref, wide_ref, PAIRS[:3])
    copies = []
    for k in range(HALF // UNIT):
        rows = pl.ds(k * UNIT, UNIT)
        update = dot(dec_rows_ref[...], wide_ref[k])
        update_ref[rows] = update
        new_ref[rows] = (weight_ref[rows].astype(F32) - RATE * update).astype(BF)
        for i, (a, b) in enumerate(((update_ref, update_hbm), (new_ref, new_hbm))):
            copy = pltpu.make_async_copy(a.at[rows], b.at[rows], sems.at[2 * k + i])
            copy.start()
            copies.append(copy)
    for copy in copies:
        copy.wait()


def held(shape, dtype=F32):
    return pltpu.VMEM(shape, dtype)


def in_hbm(array):
    return pltpu.with_memory_space_constraint(array, pltpu.HBM)


def in_vmem(array):
    return pltpu.with_memory_space_constraint(array, pltpu.VMEM)


ANY = pl.BlockSpec(memory_space=pl.ANY)
INSIDE = pl.BlockSpec(memory_space=pltpu.VMEM)


def single(kernel, operands, specs, out_specs, out_shape, scratch, flops, nbytes, aliases={}):
    return pl.pallas_call(
        kernel,
        in_specs=specs,
        out_specs=out_specs,
        out_shape=out_shape,
        scratch_shapes=scratch,
        input_output_aliases=aliases,
        compiler_params=pltpu.CompilerParams(vmem_limit_bytes=VMEM_LIMIT),
        cost_estimate=pl.CostEstimate(flops=flops, bytes_accessed=nbytes, transcendentals=0),
    )(*operands)


COEFFS = jax.ShapeDtypeStruct((BANDS * ROWS_KEPT // 128, 128), F32)


def shift(axes, by):
    pairs = []
    for z in range(4):
        for y in range(4):
            for x in range(4):
                for core in range(2):
                    to = [z, y, x]
                    to[axes[core]] = (to[axes[core]] + by) % 4
                    pairs.append(((z * 16 + y * 4 + x) * 2 + core, (to[0] * 16 + to[1] * 4 + to[2]) * 2 + core))
    return pairs


def from_axis(x, axes, order=(3, 2, 1)):
    return [lax.ppermute(x, ("rep", "fsdp"), shift(axes, by)) for by in order]


def add_up(x, parts, beside):
    (a, b, c), _ = lax.optimization_barrier((parts, beside))
    return (x + c) + (a + b)


ORDERS = ((2, 1), (1, 0), (0, 2))
SWAP = ((0, 1), (1, 0))


def shards(acts, cotangent, weight, momentum):
    core = lax.axis_index("fsdp").astype(jnp.int32)
    enc_kv, enc_kv_cols = encoder_rows(KV), encoder_cols(KV)
    enc_rows, enc_cols = encoder_rows(UNIT), encoder_cols(UNIT)
    rows = (HALF, KV)
    SCALAR = pl.BlockSpec(memory_space=pltpu.SMEM)
    dma = lambda n: pltpu.SemaphoreType.DMA((n,))

    theirs, cot, z, acts_theirs, early = single(
        theirs_kernel,
        [(1 - core).reshape(1), *map(in_hbm, (cotangent, enc_kv, enc_cols, acts, momentum))],
        [SCALAR] + [ANY] * 5, [INSIDE] * 5,
        [COEFFS, held((TOK, KV), BF), held((2 * BANDS, TOK), BF), held((TOK, HALF), BF), held((EARLY, KV))],
        [held(enc_kv.shape, BF), held(enc_cols.shape, BF), dma(4 + len(THEIRS_CHUNKS))],
        2 * TOK * HALF * 192, 6_500_000,
    )
    got = lax.ppermute(theirs, "fsdp", SWAP)
    mine, acts_mine, late = single(
        mine_kernel,
        [core.reshape(1), in_vmem(z), in_vmem(early), enc_rows, enc_kv_cols, enc_cols, *map(in_hbm, (acts, momentum))],
        [SCALAR] + [INSIDE] * 5 + [ANY] * 2, [INSIDE] * 3,
        [COEFFS, held((TOK, HALF), BF), held((HALF - EARLY, KV))], [dma(len(MINE_ORDER))],
        2 * TOK * HALF * 300, 11_000_000,
    )
    coeffs, acts_theirs, cot_theirs = lax.optimization_barrier((mine + got, acts_theirs, cot))
    acts_got, cot_got = (lax.ppermute(x, "fsdp", SWAP) for x in (acts_theirs, cot_theirs))

    parts = from_axis(coeffs, ORDERS[0])
    own = single(
        own_kernel, [coeffs, *map(in_vmem, (cot, acts_mine, early, late))], [ANY] + [INSIDE] * 4,
        INSIDE, held(rows), [], 2 * TOK * HALF * KV, 12_000_000,
    )
    total = add_up(coeffs, parts, own)
    dec_rows = decoder_rows(PAIRS)
    momentum_shape = jax.ShapeDtypeStruct((1, HALF, KV), F32)
    others = [in_vmem(x) for x in (own, cot_got, acts_got)]
    new_momentum, wide = single(
        first_rows_kernel, [total, decoder_cols(PAIRS), dec_rows, coeffs, *others],
        [ANY] + [INSIDE] * 6, [ANY, INSIDE], [momentum_shape, held((HALF // UNIT, 6 * KEPT, KV), BF)],
        [held((FIRST, KV)), dma(FIRST // UNIT)], 2 * TOK * FIRST * 700, 12_000_000,
    )
    total = add_up(total, from_axis(total, ORDERS[1]), new_momentum)
    new_momentum = single(
        last_rows_kernel, [total, new_momentum, in_vmem(wide), dec_rows, *others],
        [ANY] * 2 + [INSIDE] * 5, ANY, momentum_shape,
        [held((HALF - FIRST, KV)), dma((HALF - FIRST) // UNIT)], 2 * TOK * (HALF - FIRST) * 700, 8_000_000,
        {1: 0},
    )
    total = add_up(total, from_axis(total, ORDERS[2], (3, 1, 2)), new_momentum)

    update, new_weight = single(
        update_kernel, [decoder_cols(PAIRS[:3]), decoder_rows(PAIRS[:3]), total, weight],
        [INSIDE] * 4, [ANY] * 2, [jax.ShapeDtypeStruct(rows, F32), jax.ShapeDtypeStruct(rows, BF)],
        [held((HALF // UNIT, 3 * KEPT, KV), BF), held(rows), held(rows, BF), dma(2 * HALF // UNIT)],
        2 * HALF * KV * 400, 11_000_000,
    )
    return new_momentum, update, new_weight


def solution(mesh):
    in_specs = (
        P(("rep", "fsdp"), None),
        P(("rep", "fsdp"), None),
        P("fsdp", None),
        P("rep", "fsdp", None),
    )
    out_specs = (P("rep", "fsdp", None), P("fsdp", None), P("fsdp", None))
    return jax.shard_map(shards, mesh=mesh, in_specs=in_specs, out_specs=out_specs, check_vma=False)
```

```python
import jax
import jax.numpy as jnp
import ml_dtypes
import numpy as np
from jax import lax
from jax.experimental import pallas as pl
from jax.experimental.pallas import tpu as pltpu
from jax.sharding import PartitionSpec as P

SPAN = 64
KEEP = 8
BETA = 0.9
RATE = 0.02

TOK = 1024
KV = 512
HALF = 2560
UNIT = 256
KEPT = UNIT // SPAN * KEEP
BANDS = KV // SPAN * KEEP
ROWS_KEPT = HALF // SPAN * KEEP

THEIRS_CHUNKS = ((0, 512), (512, 1024), (1024, 1536), (1536, 2048), (2048, 2560))
MINE_CHUNKS = ((0, 1280), (1280, 2560))
MINE_ORDER = (("m", 0), ("m", 1), ("a", 0), ("m", 2), ("m", 3), ("a", 1), ("m", 4))
MOM_STEP = 512
EARLY = 1024
FIRST = 1792
VMEM_LIMIT = 24 * 1024 * 1024

BF = jnp.bfloat16
F32 = jnp.float32


def dct_rows():
    freq = np.arange(KEEP)[:, None].astype(np.float64)
    cell = np.arange(SPAN)[None, :].astype(np.float64)
    scale = np.where(freq == 0, np.sqrt(1.0 / SPAN), np.sqrt(2.0 / SPAN))
    return (scale * np.cos(np.pi * (2.0 * cell + 1.0) * freq / (2.0 * SPAN))).astype(np.float32)


def basis_terms(size):
    out, rest = [], np.kron(np.eye(size // SPAN, dtype=np.float32), dct_rows())
    for _ in range(3):
        part = rest.astype(ml_dtypes.bfloat16)
        out.append(part)
        rest = rest - part.astype(np.float32)
    return out


PAIRS = ((0, 0), (0, 1), (1, 0), (1, 1), (0, 2), (2, 0))


def encoder_rows(size):
    return jnp.asarray(np.concatenate(basis_terms(size), axis=0))


def encoder_cols(size):
    return jnp.asarray(np.concatenate([t.T for t in basis_terms(size)], axis=1))


def decoder_cols(pairs):
    t = basis_terms(KV)
    return jnp.asarray(np.concatenate([t[j] for _, j in pairs], axis=0))


def decoder_rows(pairs):
    t = basis_terms(UNIT)
    return jnp.asarray(np.concatenate([t[i].T for i, _ in pairs], axis=1))


def pack(coeffs, out_ref):
    out_ref[:64] = coeffs[:, :128]
    out_ref[64:128] = coeffs[:, 128:256]
    out_ref[128:] = jnp.concatenate([coeffs[:32, 256:], coeffs[32:, 256:]], axis=1)


def unpack(packed):
    rest = jnp.concatenate([packed[128:, :64], packed[128:, 64:]], axis=0)
    return jnp.concatenate([packed[:64], packed[64:128], rest], axis=1)


def split(x):
    hi = x.astype(BF)
    rest = x - hi.astype(F32)
    mid = rest.astype(BF)
    lo = (rest - mid.astype(F32)).astype(BF)
    return hi, mid, lo


def dot(a, b, dims=((1,), (0,))):
    return lax.dot_general(a, b, (dims, ((), ())), preferred_element_type=F32)


def cross(product, rows, cols):
    total = None
    for i, j in reversed(PAIRS):
        piece = product[i * rows : (i + 1) * rows, j * cols : (j + 1) * cols]
        total = piece if total is None else total + piece
    return total


class Arrivals:
    def __init__(self, pairs, sems, ahead):
        self.copies = [pltpu.make_async_copy(a, b, sems.at[k]) for k, (a, b) in enumerate(pairs)]
        self.started, self.waited, self.ahead = 0, 0, ahead
        self.fill()

    def fill(self):
        while self.started < min(len(self.copies), self.waited + self.ahead):
            self.copies[self.started].start()
            self.started += 1

    def next(self):
        self.copies[self.waited].wait()
        self.waited += 1
        self.fill()


def encode_chunk(g, enc_cols):
    t = split(g)
    pieces = []
    for k in range(g.shape[1] // UNIT):
        stacked = jnp.concatenate([x[:, k * UNIT : (k + 1) * UNIT] for x in t], axis=0)
        pieces.append(cross(dot(stacked, enc_cols), BANDS, KEPT))
    return pieces


def momentum_rows(early_ref, late_ref, start):
    if start < EARLY:
        return early_ref[start : start + UNIT]
    return late_ref[start - EARLY : start - EARLY + UNIT]


def acts_copies(acts_hbm, acts_ref, half, chunks):
    pairs = []
    for lo, hi in chunks:
        start = pl.multiple_of(half * HALF + lo, UNIT)
        pairs.append((acts_hbm.at[:, pl.ds(start, hi - lo)], acts_ref.at[:, lo:hi]))
    return pairs


def encode_acts(z_ref, acts_ref, lo, hi):
    g = dot(z_ref[...], acts_ref[:, lo:hi])
    return g[BANDS:] + g[:BANDS]


def theirs_kernel(
    half, cot_hbm, enc_kv_hbm, enc_cols_hbm, acts_hbm, mom_hbm,
    theirs_ref, cot_ref, z_ref, acts_ref, mom_ref, enc_kv_ref, enc_cols_ref, sems,
):
    pairs = [(enc_kv_hbm, enc_kv_ref), (cot_hbm, cot_ref), (enc_cols_hbm, enc_cols_ref)]
    pairs += acts_copies(acts_hbm, acts_ref, half[0], THEIRS_CHUNKS)
    pairs.append((mom_hbm.at[0, :EARLY], mom_ref))
    arrivals = Arrivals(pairs, sems, 5)
    arrivals.next()
    arrivals.next()

    z = dot(enc_kv_ref[...], cot_ref[...], ((1,), (1,)))
    z_ref[...] = jnp.concatenate(split(z[2 * BANDS :] + z[BANDS : 2 * BANDS] + z[:BANDS])[:2], axis=0)
    arrivals.next()

    found, before = [], None
    for lo, hi in THEIRS_CHUNKS:
        arrivals.next()
        g = encode_acts(z_ref, acts_ref, lo, hi)
        if before is not None:
            found += encode_chunk(before, enc_cols_ref[...])
        before = g
    found += encode_chunk(before, enc_cols_ref[...])
    pack(jnp.concatenate(found, axis=1), theirs_ref)
    arrivals.next()


def mine_kernel(
    half, z_ref, early_ref, enc_rows_ref, enc_kv_cols_ref, enc_cols_ref, acts_hbm, mom_hbm,
    mine_ref, acts_ref, late_ref, sems,
):
    from_acts = acts_copies(acts_hbm, acts_ref, half[0], MINE_CHUNKS)
    from_mom = [
        (mom_hbm.at[0, pl.ds(start, MOM_STEP)], late_ref.at[pl.ds(start - EARLY, MOM_STEP)])
        for start in range(EARLY, HALF, MOM_STEP)
    ]
    copies = {("a", k): pair for k, pair in enumerate(from_acts)}
    copies |= {("m", EARLY // MOM_STEP + k): pair for k, pair in enumerate(from_mom)}
    arrivals = Arrivals([copies[c] for c in MINE_ORDER if c in copies], sems, 3)
    enc = enc_rows_ref[...]

    def encode_rows(start):
        m = momentum_rows(early_ref, late_ref, start)
        hi = m.astype(BF)
        a = dot(enc, hi)
        b = dot(enc[: 2 * KEPT], (m - hi.astype(F32)).astype(BF))
        return (b[KEPT:] + a[2 * KEPT :]) + (b[:KEPT] + a[KEPT : 2 * KEPT]) + a[:KEPT]

    def encode_cols(parts):
        n = len(parts) * KEPT
        terms = split(jnp.concatenate(parts, axis=0))
        return cross(dot(jnp.concatenate(terms, axis=0), enc_kv_cols_ref[...]), n, BANDS)

    found, from_rows, before = [], [], None
    for kind, k in MINE_ORDER + ((None, 0),):
        done = before
        if kind is not None:
            if (kind, k) in copies:
                arrivals.next()
            if kind == "a":
                before = kind, encode_acts(z_ref, acts_ref, *MINE_CHUNKS[k])
            else:
                before = kind, [encode_rows(k * MOM_STEP + i * UNIT) for i in range(MOM_STEP // UNIT)]
        if done is not None:
            if done[0] == "a":
                found += encode_chunk(done[1], enc_cols_ref[...])
            else:
                from_rows.append(encode_cols(done[1]))
    pack(jnp.concatenate(found, axis=1) + BETA * jnp.concatenate(from_rows, axis=0).T, mine_ref)


def own_kernel(dec_cols_ref, coeffs_ref, cot_ref, acts_ref, early_ref, late_ref, out_ref, wide_ref):
    decode_cols(unpack(coeffs_ref[...]), dec_cols_ref, wide_ref, PAIRS)
    for start in range(0, HALF, UNIT):
        rows = slice(start, start + UNIT)
        g = dot(acts_ref[:, rows], cot_ref[...], ((0,), (0,)))
        out_ref[rows] = BETA * momentum_rows(early_ref, late_ref, start) + g


def decode_cols(coeffs, dec_cols_ref, out_ref, pairs):
    t = split(coeffs)
    wide = dot(jnp.concatenate([t[i] for i, _ in pairs], axis=0), dec_cols_ref[...], ((0,), (0,)))
    w = split(wide)
    for g in range(HALF // UNIT):
        out_ref[g] = jnp.concatenate([w[j][g * KEPT : (g + 1) * KEPT] for _, j in pairs], axis=0)


def write_rows(first, last, own_ref, wide_ref, dec_rows_ref, cot_ref, acts_ref, out_hbm, out_ref, sems):
    copies = []
    for k, start in enumerate(range(first, last, UNIT)):
        rows, here = pl.ds(start, UNIT), pl.ds(start - first, UNIT)
        g = dot(acts_ref[:, rows], cot_ref[...], ((0,), (0,)))
        out_ref[here] = own_ref[rows] + g - dot(dec_rows_ref[...], wide_ref[start // UNIT])
        copy = pltpu.make_async_copy(out_ref.at[here], out_hbm.at[0, rows], sems.at[k])
        copy.start()
        copies.append(copy)
    for copy in copies:
        copy.wait()


def first_rows_kernel(
    dep, wide_ref, dec_rows_ref, own_ref, cot_ref, acts_ref, out_hbm, out_ref, sems
):
    write_rows(0, FIRST, own_ref, wide_ref, dec_rows_ref, cot_ref, acts_ref, out_hbm, out_ref, sems)


def last_rows_kernel(
    dep, before, wide_ref, dec_rows_ref, own_ref, cot_ref, acts_ref, out_hbm, out_ref, sems
):
    write_rows(FIRST, HALF, own_ref, wide_ref, dec_rows_ref, cot_ref, acts_ref, out_hbm, out_ref, sems)


def update_kernel(
    dec_cols_ref, dec_rows_ref, coeffs_ref, weight_ref, update_hbm, new_hbm, wide_ref, update_ref, new_ref, sems
):
    decode_cols(unpack(coeffs_ref[...]), dec_cols_ref, wide_ref, PAIRS[:3])
    copies = []
    for k in range(HALF // UNIT):
        rows = pl.ds(k * UNIT, UNIT)
        update = dot(dec_rows_ref[...], wide_ref[k])
        update_ref[rows] = update
        new_ref[rows] = (weight_ref[rows].astype(F32) - RATE * update).astype(BF)
        for i, (a, b) in enumerate(((update_ref, update_hbm), (new_ref, new_hbm))):
            copy = pltpu.make_async_copy(a.at[rows], b.at[rows], sems.at[2 * k + i])
            copy.start()
            copies.append(copy)
    for copy in copies:
        copy.wait()


def held(shape, dtype=F32):
    return pltpu.VMEM(shape, dtype)


def in_hbm(array):
    return pltpu.with_memory_space_constraint(array, pltpu.HBM)


def in_vmem(array):
    return pltpu.with_memory_space_constraint(array, pltpu.VMEM)


ANY = pl.BlockSpec(memory_space=pl.ANY)
INSIDE = pl.BlockSpec(memory_space=pltpu.VMEM)


def single(kernel, operands, specs, out_specs, out_shape, scratch, flops, nbytes, aliases={}):
    return pl.pallas_call(
        kernel,
        in_specs=specs,
        out_specs=out_specs,
        out_shape=out_shape,
        scratch_shapes=scratch,
        input_output_aliases=aliases,
        compiler_params=pltpu.CompilerParams(vmem_limit_bytes=VMEM_LIMIT),
        cost_estimate=pl.CostEstimate(flops=flops, bytes_accessed=nbytes, transcendentals=0),
    )(*operands)


COEFFS = jax.ShapeDtypeStruct((BANDS * ROWS_KEPT // 128, 128), F32)


def shift(axes, by):
    pairs = []
    for z in range(4):
        for y in range(4):
            for x in range(4):
                for core in range(2):
                    to = [z, y, x]
                    to[axes[core]] = (to[axes[core]] + by) % 4
                    pairs.append(((z * 16 + y * 4 + x) * 2 + core, (to[0] * 16 + to[1] * 4 + to[2]) * 2 + core))
    return pairs


def from_axis(x, axes, order=(3, 2, 1)):
    return [lax.ppermute(x, ("rep", "fsdp"), shift(axes, by)) for by in order]


def add_up(x, parts, beside):
    (a, b, c), _ = lax.optimization_barrier((parts, beside))
    return (x + c) + (a + b)


ORDERS = ((2, 1), (1, 0), (0, 2))
SWAP = ((0, 1), (1, 0))


def shards(acts, cotangent, weight, momentum):
    core = lax.axis_index("fsdp").astype(jnp.int32)
    enc_kv, enc_kv_cols = encoder_rows(KV), encoder_cols(KV)
    enc_rows, enc_cols = encoder_rows(UNIT), encoder_cols(UNIT)
    rows = (HALF, KV)
    SCALAR = pl.BlockSpec(memory_space=pltpu.SMEM)
    dma = lambda n: pltpu.SemaphoreType.DMA((n,))

    theirs, cot, z, acts_theirs, early = single(
        theirs_kernel,
        [(1 - core).reshape(1), *map(in_hbm, (cotangent, enc_kv, enc_cols, acts, momentum))],
        [SCALAR] + [ANY] * 5, [INSIDE] * 5,
        [COEFFS, held((TOK, KV), BF), held((2 * BANDS, TOK), BF), held((TOK, HALF), BF), held((EARLY, KV))],
        [held(enc_kv.shape, BF), held(enc_cols.shape, BF), dma(4 + len(THEIRS_CHUNKS))],
        2 * TOK * HALF * 192, 6_500_000,
    )
    got = lax.ppermute(theirs, "fsdp", SWAP)
    mine, acts_mine, late = single(
        mine_kernel,
        [core.reshape(1), in_vmem(z), in_vmem(early), enc_rows, enc_kv_cols, enc_cols, *map(in_hbm, (acts, momentum))],
        [SCALAR] + [INSIDE] * 5 + [ANY] * 2, [INSIDE] * 3,
        [COEFFS, held((TOK, HALF), BF), held((HALF - EARLY, KV))], [dma(len(MINE_ORDER))],
        2 * TOK * HALF * 300, 11_000_000,
    )
    coeffs, acts_theirs, cot_theirs = lax.optimization_barrier((mine + got, acts_theirs, cot))
    acts_got, cot_got = (lax.ppermute(x, "fsdp", SWAP) for x in (acts_theirs, cot_theirs))

    parts = from_axis(coeffs, ORDERS[0])
    own, wide = single(
        own_kernel, [decoder_cols(PAIRS), coeffs, *map(in_vmem, (cot, acts_mine, early, late))], [INSIDE] * 6,
        [INSIDE] * 2, [held(rows), held((HALF // UNIT, 6 * KEPT, KV), BF)], [], 2 * TOK * HALF * KV, 12_000_000,
    )
    total = add_up(coeffs, parts, own)
    dec_rows = decoder_rows(PAIRS)
    momentum_shape = jax.ShapeDtypeStruct((1, HALF, KV), F32)
    others = [in_vmem(x) for x in (own, cot_got, acts_got)]
    new_momentum = single(
        first_rows_kernel, [total, in_vmem(wide), dec_rows, *others],
        [ANY] + [INSIDE] * 5, ANY, momentum_shape,
        [held((FIRST, KV)), dma(FIRST // UNIT)], 2 * TOK * FIRST * 700, 12_000_000,
    )
    total = add_up(total, from_axis(total, ORDERS[1]), new_momentum)
    new_momentum = single(
        last_rows_kernel, [total, new_momentum, in_vmem(wide), dec_rows, *others],
        [ANY] * 2 + [INSIDE] * 5, ANY, momentum_shape,
        [held((HALF - FIRST, KV)), dma((HALF - FIRST) // UNIT)], 2 * TOK * (HALF - FIRST) * 700, 8_000_000,
        {1: 0},
    )
    total = add_up(total, from_axis(total, ORDERS[2], (3, 1, 2)), new_momentum)

    update, new_weight = single(
        update_kernel, [decoder_cols(PAIRS[:3]), decoder_rows(PAIRS[:3]), total, weight],
        [INSIDE] * 4, [ANY] * 2, [jax.ShapeDtypeStruct(rows, F32), jax.ShapeDtypeStruct(rows, BF)],
        [held((HALF // UNIT, 3 * KEPT, KV), BF), held(rows), held(rows, BF), dma(2 * HALF // UNIT)],
        2 * HALF * KV * 400, 11_000_000,
    )
    return new_momentum, update, new_weight


def solution(mesh):
    in_specs = (
        P(("rep", "fsdp"), None),
        P(("rep", "fsdp"), None),
        P("fsdp", None),
        P("rep", "fsdp", None),
    )
    out_specs = (P("rep", "fsdp", None), P("fsdp", None), P("fsdp", None))
    return jax.shard_map(shards, mesh=mesh, in_specs=in_specs, out_specs=out_specs, check_vma=False)
```
